512 devices in a mesh: wave: 128 (over x, z, core), basin: 4 (over y).
Axes of the slice: x: 4, y: 4, z: 16, core: 2. Of those that a mesh axis runs over, the one named last changes fastest.
Arguments:
- spectra: bfloat16 [16, 2, 1280, 1280], P('basin', None, 'wave'), may hold values from -6 to 6
- legendre: bfloat16 [1280, 1280, 128], P('wave'), may hold values from -0.15625 to 0.15625
- wave_numbers: int32 [1280], P('wave'), may hold values from 0 to 1279, each once
- block_index: int32 [128, 1024], P('wave'), may hold values from 0 to 159
- block_weights: bfloat16 [128, 1024, 128], P('wave'), may hold values from 0.019897461 to 0.19921875
- basin_index: int32 [128, 1024], P('wave'), may hold values from 0 to 65535, as said below
Outputs:
- grid_fields: bfloat16 [16, 2, 128, 10240], P('basin', None, 'wave')
- basin_sums: float32 [16, 65536], P(None, ('wave', 'basin'))
The draws below stay inside these ranges and needn't reach their ends.
Inputs may be any that keep to these rules, and one draw needn't show every extreme that they name: `basin_index`: the owner of basin b along wave is b // 512; the 1024 rows of one latitude pair name basins of exactly 64 owners, 16 rows for each.
All inputs are finite; a program needn't handle non-finite values.
Results may differ from the reference program's by a relative error of at most 0.0061.
Values may be sent and summed in bfloat16 or wider, within the bound.
A program may use at most 128 MiB of HBM per device.

```python
import math
import jax
import jax.numpy as jnp
from jax import lax

F_TOT = 16
M_TOT = 1280
NN = 1280
LATS = 128
NLON = 10240
LB = 128
BLOCK = 128
NBLK = 160
NNZ_LAT = 1024
CAP = 16
GROUPS = 64
BPW = 512
NBASIN = 65536
N_WAVE = 128


def draw_basin_index(key, part):
    key = jax.random.fold_in(key, 7)
    key_busy, key_score, key_order, key_local = jax.random.split(key, 4)
    busy = jax.random.permutation(key_busy, N_WAVE) < max(1, N_WAVE // 4)
    score = jax.random.randint(key_score, (LATS, N_WAVE), 0, 1 << 12) + jnp.where(busy, 1 << 11, 0)
    score = score * N_WAVE + jnp.arange(N_WAVE, dtype=jnp.int32)[None, :]
    unused, owners = lax.top_k(score, GROUPS)
    dest = jnp.repeat(owners, CAP, axis=1)
    order_key = jax.random.randint(key_order, (LATS, NNZ_LAT), 0, 1 << 16) * NNZ_LAT + jnp.arange(NNZ_LAT, dtype=jnp.int32)[None, :]
    order = jnp.argsort(order_key, axis=1, stable=True)
    dest = jnp.take_along_axis(dest, order, axis=1)
    local = jax.random.randint(key_local, (LATS, NNZ_LAT), 0, BPW)
    return (dest * BPW + local).astype(jnp.int32)


def set_ends(values, key, smallest, high):
    spot = [jax.random.randint(jax.random.fold_in(key, axis), (), 0, length) for axis, length in enumerate(values.shape)]
    longest = values.shape.index(max(values.shape))
    next_to = spot[:longest] + [(spot[longest] + 1) % values.shape[longest]] + spot[longest + 1:]
    return values.at[tuple(spot)].set(smallest).at[tuple(next_to)].set(high)


def shard_levels(own_key, dims, shards, smallest, top_value):
    def one(axis_at, shards_of):
        draws = jax.random.uniform(jax.random.fold_in(jax.random.fold_in(own_key, 6), axis_at), (shards_of,), jnp.float32, smallest / len(shards), top_value / len(shards))
        return jnp.repeat(jnp.exp(draws), dims[axis_at] // shards_of).reshape((-1,) + (1,) * (len(dims) - axis_at - 1))

    factor_of = one(*shards[0])
    for cut in shards[1:]:
        factor_of = factor_of * one(*cut)
    return factor_of


def gaussian(own_key, extent, width, most, cuts=(), kind=jnp.bfloat16):
    loudness = shard_levels(own_key, extent, cuts, -0.22, 0.18) if cuts else 1.0
    array = jax.random.normal(own_key, extent, jnp.float32) * width * loudness
    return jnp.minimum(jnp.maximum(array, -most), most).astype(kind)


def setup_inputs(seed: int = 0) -> dict:
    splits = jax.random.split(jax.random.key(seed), 7)
    return {
        "spectra": gaussian(splits[0], (F_TOT, 2, M_TOT, NN), 1.0, 6.0, ((0, 4), (2, 128))),
        "legendre": gaussian(splits[1], (M_TOT, NN, LATS), NN ** -0.5, 0.15625, ((0, 128),)),
        "wave_numbers": jax.random.permutation(splits[2], M_TOT).astype(jnp.int32),
        "block_index": set_ends(jax.random.randint(splits[3], (LATS, NNZ_LAT), 0, NBLK), jax.random.fold_in(splits[3], 1), 0, NBLK - 1).astype(jnp.int32),
        "block_weights": jnp.clip(jnp.exp(math.log(0.19921875) - 2.3038113 * jax.random.uniform(splits[4], (LATS, NNZ_LAT, BLOCK), jnp.float32) ** shard_levels(splits[4], (LATS, NNZ_LAT, BLOCK), ((0, 128),), -0.2, 0.2)), 0.019897461, 0.19921875).astype(jnp.bfloat16),
        "basin_index": draw_basin_index(jax.random.fold_in(splits[6], 71), 0),
    }


def reference(spectra, legendre, wave_numbers, block_index, block_weights, basin_index):
    sign = jnp.where(jnp.arange(NN) % 2 == 0, 1.0, -1.0).astype(jnp.bfloat16)

    def column(pair):
        coeffs, table = pair
        rows = coeffs.reshape(F_TOT * 2, NN)
        both = jnp.concatenate([rows, rows * sign], axis=0)
        return jnp.dot(both, table, preferred_element_type=jnp.float32).astype(jnp.bfloat16)
    cols = lax.map(column, (jnp.moveaxis(spectra, 2, 0), legendre))
    cols = cols.reshape(M_TOT, 2, F_TOT, 2, LATS)
    north_south = jnp.transpose(cols, (2, 1, 4, 3, 0))
    blocks = NLON // LB
    wavenum = wave_numbers.astype(jnp.int32)
    starts = jnp.arange(blocks, dtype=jnp.int32) * LB
    theta = (wavenum[None, :] * starts[:, None] % NLON).astype(jnp.float32) * (2.0 * math.pi / NLON)
    cos_a = jnp.cos(theta)
    sin_a = jnp.sin(theta)
    weight = jnp.where(wavenum == 0, 1.0, 2.0).astype(jnp.float32)
    offsets = jnp.arange(LB, dtype=jnp.int32)
    phi = (wavenum[:, None] * offsets[None, :] % NLON).astype(jnp.float32) * (2.0 * math.pi / NLON)
    basis = jnp.concatenate([jnp.cos(phi), -jnp.sin(phi)], axis=0).astype(jnp.bfloat16)
    scale = 1.0 / math.sqrt(2.0 * M_TOT)

    def transform(field):
        rows = field.reshape(2 * LATS, 2, M_TOT).astype(jnp.float32)
        g_re = rows[:, 0, :]
        g_im = rows[:, 1, :]
        turned_re = (weight * (g_re[None] * cos_a[:, None] - g_im[None] * sin_a[:, None])).astype(jnp.bfloat16)
        turned_im = (weight * (g_re[None] * sin_a[:, None] + g_im[None] * cos_a[:, None])).astype(jnp.bfloat16)
        turned = jnp.concatenate([turned_re, turned_im], axis=2).reshape(blocks * 2 * LATS, 2 * M_TOT)
        out = jnp.dot(turned, basis, preferred_element_type=jnp.float32) * scale
        out = out.reshape(blocks, 2 * LATS, LB).transpose(1, 0, 2).reshape(2, LATS, NLON)
        return out.astype(jnp.bfloat16)
    grid_fields = lax.map(transform, north_south)
    index = jnp.broadcast_to(block_index.astype(jnp.int32)[:, :, None], (LATS, NNZ_LAT, BLOCK))
    weights = block_weights.astype(jnp.float32)
    basins = basin_index.reshape(-1).astype(jnp.int32)

    def pool(field_grid):
        rows = jnp.moveaxis(field_grid, 0, 1).reshape(LATS, NBLK, BLOCK)
        picked = jnp.take_along_axis(rows, index, axis=1).astype(jnp.float32)
        values = lax.optimization_barrier(jnp.sum(picked * weights, axis=2))
        return jax.ops.segment_sum(values.reshape(-1), basins, num_segments=NBASIN)
    basin_sums = lax.map(pool, grid_fields)
    return (grid_fields, basin_sums)
```

```python
import functools
import math

import jax
import jax.numpy as jnp
from jax import lax
from jax.experimental import pallas as pl
from jax.experimental.pallas import tpu as pltpu
from jax.sharding import PartitionSpec as P

NLON = 10240
LB = 128
BLOCK = 128
SLOTS = 16
BPW_BITS = 9
BPW = 1 << BPW_BITS
MESH = pl.DeviceIdType.MESH
F32 = jnp.float32
BF16 = jnp.bfloat16

COS_C = [(-1) ** n * math.pi ** (2 * n) / math.factorial(2 * n) for n in range(7)]
SIN_C = [(-1) ** n * math.pi ** (2 * n + 1) / math.factorial(2 * n + 1) for n in range(6)]


def cos_sin(r, turn):
    r = r - turn * jnp.floor(r * (1.0 / turn) + 0.5)
    y = r * (1.0 / turn)
    yy = y * y
    c = jnp.full_like(yy, COS_C[6])
    for k in range(5, -1, -1):
        c = c * yy + COS_C[k]
    s = jnp.full_like(yy, SIN_C[5])
    for k in range(4, -1, -1):
        s = s * yy + SIN_C[k]
    s = s * y
    return 1.0 - 2.0 * (s * s), 2.0 * (s * c)


def partner(k, me, nw):
    if nw != 128:
        return lax.rem(me + 1 + k, nw)
    x, z, c = me // 32, (me // 2) % 16, me % 2
    i, r = k // 8, k % 8
    zd = jnp.where(i % 2 == 0, 8 - i // 2, 8 + (i + 1) // 2)
    rx = r // 2
    xd = jnp.where(rx == 0, 2, jnp.where(rx == 1, 1, jnp.where(rx == 2, 3, 0)))
    cd = 1 - r % 2
    return (lax.rem(x + xd, 4) * 16 + lax.rem(z + zd, 16)) * 2 + lax.rem(c + cd, 2)


def iota(shape, dim):
    return lax.broadcasted_iota(jnp.int32, shape, dim)


def kernel(nw, ng, spec_ref, leg_hbm, wn_ref, blk_ref, wgt_ref, bas_ref,
           grid_hbm, sums_ref,
           leg, sa, ra, sb, rb, sd, rd, tu, ba, ws, one, vs, gr, pm,
           leg_sem, grid_sem, sa_sem, ra_sem, sb_sem, rb_sem, sd_sem, rd_sem):
    me, y = lax.axis_index("wave"), lax.axis_index("basin")
    mloc = leg.shape[0]
    nb, eb = bas_ref.shape
    nq = SLOTS * nw

    barrier = pltpu.get_barrier_semaphore()

    def greet(k, carry):
        pl.semaphore_signal(barrier, inc=1, device_id=(partner(k, me, nw), y), device_id_type=MESH)
        return carry

    lax.fori_loop(0, nw - 1, greet, 0)
    for k in range(1, ng):
        pl.semaphore_signal(barrier, inc=1, device_id=(me, lax.rem(y + k, ng)), device_id_type=MESH)

    for m in range(mloc):
        pltpu.make_async_copy(leg_hbm.at[m], leg.at[m], leg_sem.at[m]).start()

    bas = bas_ref[...]
    owner = bas >> BPW_BITS
    local = bas & (BPW - 1)
    upper = (iota((eb, eb), 0) < iota((eb, eb), 1)).astype(F32).astype(BF16)
    owned = [(owner[i:i + 1] == iota((nw, eb), 0)).astype(F32) for i in range(nb)]
    before = jnp.zeros((nw, 1), F32)
    ranks = []
    for i in range(nb):
        inside = jnp.dot(owned[i].astype(BF16), upper, preferred_element_type=F32)
        ranks.append(jnp.sum(owned[i] * (inside + before), axis=0, keepdims=True))
        before = before + jnp.sum(owned[i], axis=1, keepdims=True)
    lane = iota((128, eb), 0)
    where_to = jnp.zeros((nw, 128), F32)
    for i in range(nb):
        high = (local[i:i + 1] >> 7).astype(F32)
        low = (local[i:i + 1] & 127).astype(F32)
        rank = ranks[i].astype(jnp.int32)
        named = jnp.where(lane == rank + 96, high, 0.0) + jnp.where(lane == rank + 112, low, 0.0)
        where_to = where_to + lax.dot_general(
            owned[i].astype(BF16), named.astype(BF16), (((1,), (1,)), ((), ())),
            preferred_element_type=F32)
    rank_rows = jnp.concatenate(ranks, axis=0)
    place = rank_rows * float(nw) + owner.astype(F32)
    place_cols = jnp.transpose(place)

    ncoef = spec_ref.shape[3]
    odd = lax.rem(iota((8, ncoef), 1), 2) == 1
    sums = []
    for m in range(mloc):
        rows = jnp.concatenate([spec_ref[f, m].astype(F32) for f in range(4)], axis=0)
        both = jnp.concatenate([rows, jnp.where(odd, -rows, rows)], axis=0).astype(BF16)
        pltpu.make_async_copy(leg_hbm.at[m], leg.at[m], leg_sem.at[m]).wait()
        sums.append(jnp.dot(both, leg[m], preferred_element_type=F32))
    sums = jnp.concatenate(sums, axis=0)
    if mloc * 16 % 128:
        sums = jnp.concatenate([sums, jnp.zeros((256 - mloc * 16, nw), F32)], axis=0)
    by_lat = jnp.transpose(sums).astype(BF16)
    src = iota((256, 256), 0)
    dst = iota((256, 256), 1)
    r_of, lane_of = dst >> 7, dst & 127
    m_of, f_of, h_of = lane_of >> 3, (lane_of >> 1) & 3, lane_of & 1
    pick = (src == m_of * 16 + h_of * 8 + f_of * 2 + r_of) & (lane_of < mloc * 8)
    ordered = jnp.dot(by_lat, pick.astype(F32).astype(BF16), preferred_element_type=F32)
    lane = iota((1, 128), 1)
    numbers = jnp.zeros((1, 128), F32)
    for m in range(mloc):
        wn = wn_ref[m]
        numbers = numbers + jnp.where(lane == 80 + m, (wn >> 7).astype(F32), 0.0)
        numbers = numbers + jnp.where(lane == 96 + m, (wn & 127).astype(F32), 0.0)
    part_re = ordered[:, :128] + numbers
    part_im = ordered[:, 128:] + where_to
    sa[...] = jnp.concatenate([part_re[:, None, :], part_im[:, None, :]], axis=1).astype(BF16)

    pl.semaphore_wait(barrier, nw - 1 + ng - 1)

    def send_a(k, carry):
        to = partner(k, me, nw)
        pltpu.make_async_remote_copy(
            src_ref=sa.at[pl.ds(to, 1)], dst_ref=ra.at[pl.ds(me, 1)], send_sem=sa_sem,
            recv_sem=ra_sem, device_id=(to, y), device_id_type=MESH).start()
        return carry

    lax.fori_loop(0, nw - 1, send_a, 0)
    ra[pl.ds(me, 1)] = sa[pl.ds(me, 1)]

    ext = jnp.concatenate(
        [jnp.concatenate([blk_ref[i:i + 1].astype(F32), jnp.zeros((15, eb), F32)], axis=0)
         for i in range(nb)], axis=1)
    turned_w = jnp.concatenate(
        [jnp.transpose(wgt_ref[i * eb:(i + 1) * eb].astype(F32)) for i in range(nb)], axis=1)
    left = jnp.concatenate([turned_w, ext], axis=0).astype(BF16)
    for i in range(nb):
        col = jnp.broadcast_to(place_cols[:, i:i + 1], (eb, 128 if nq >= 128 else nq))
        for c in range(max(1, nq // 128)):
            spot = (iota(col.shape, 1) + c * 128).astype(F32)
            pm[i * eb:(i + 1) * eb, c * 128:c * 128 + col.shape[1]] = jnp.where(
                col == spot, 1.0, 0.0).astype(BF16)
    qc = min(256, nq)
    for c in range(nq // qc):
        ws[:, c * qc:(c + 1) * qc] = jnp.dot(
            left, pm[:, c * qc:(c + 1) * qc], preferred_element_type=F32).astype(BF16)
    vs[...] = jnp.zeros(vs.shape, F32)

    pltpu.make_async_copy(sa.at[pl.ds(0, nw - 1)], ra.at[pl.ds(0, nw - 1)], ra_sem).wait()

    got = ra[...].astype(F32)
    re, im = got[:, 0, :], got[:, 1, :]
    re_t, im_t = jnp.transpose(re), jnp.transpose(im)
    m_rows = re_t[80:96] * 128.0 + re_t[96:112]
    a_of = (iota((80, nw), 0) >> 1).astype(F32)
    parity = lax.rem(iota((8, nw), 0), 2) == 0
    ncols = mloc * nw
    b_of = iota((nw, LB), 1).astype(F32)
    for m in range(mloc):
        number = m_rows[m:m + 1]
        weight = jnp.where(number == 0.0, 1.0, 2.0)
        cos_a, sin_a = cos_sin(number * a_of, 80.0)
        cos_a, sin_a = cos_a.reshape(10, 8, nw), sin_a.reshape(10, 8, nw)
        g_re = re_t[m * 8:(m + 1) * 8] * weight
        g_im = im_t[m * 8:(m + 1) * 8] * weight
        for f in range(4):
            fr = jnp.where(parity, g_re[2 * f:2 * f + 1], g_re[2 * f + 1:2 * f + 2])[None]
            fi = jnp.where(parity, g_im[2 * f:2 * f + 1], g_im[2 * f + 1:2 * f + 2])[None]
            t_re = (fr * cos_a - fi * sin_a).reshape(80, nw)
            t_im = (fr * sin_a + fi * cos_a).reshape(80, nw)
            tu[f * 80:(f + 1) * 80, m * nw:(m + 1) * nw] = t_re.astype(BF16)
            tu[f * 80:(f + 1) * 80, ncols + m * nw:ncols + (m + 1) * nw] = t_im.astype(BF16)
        column = re[:, 80 + m:81 + m] * 128.0 + re[:, 96 + m:97 + m]
        cos_b, sin_b = cos_sin(column * b_of, float(NLON))
        flip = 1.0 - 2.0 * (column - 2.0 * jnp.floor(column * 0.5))
        rows = slice(m * nw, (m + 1) * nw)
        ba[rows, :128] = cos_b.astype(BF16)
        ba[rows, 128:] = (cos_b * flip).astype(BF16)
        rows = slice(ncols + m * nw, ncols + (m + 1) * nw)
        ba[rows, :128] = (-sin_b).astype(BF16)
        ba[rows, 128:] = (-sin_b * flip).astype(BF16)
    scale = 1.0 / math.sqrt(2.0 * ncols)
    for f in range(4):
        lines = jnp.dot(tu[f * 80:(f + 1) * 80], ba[...], preferred_element_type=F32) * scale
        gr[f, :80] = lines[:, :128].astype(BF16)
        gr[f, 80:] = lines[:, 128:].astype(BF16)

    row = iota((160, qc), 0)
    block_of = (row & 1) * 80 + (row >> 1)
    block_of = block_of.astype(F32)
    for c in range(nq // qc):
        cols = slice(c * qc, (c + 1) * qc)
        hit = block_of == ws[128:129, cols].astype(F32)
        for f in range(4):
            prod = jnp.dot(gr[f], ws[:128, cols], preferred_element_type=F32)
            val = jnp.sum(jnp.where(hit, prod, 0.0), axis=0, keepdims=True)
            for j in range(qc // nw):
                s = c * (qc // nw) + j
                vs[s * 4 + f:s * 4 + f + 1, :nw] = val[:, j * nw:(j + 1) * nw]
    sb[...] = jnp.transpose(vs[...])

    def send_b(k, carry):
        to = partner(k, me, nw)
        pltpu.make_async_remote_copy(
            src_ref=sb.at[pl.ds(to, 1)], dst_ref=rb.at[pl.ds(me, 1)], send_sem=sb_sem,
            recv_sem=rb_sem, device_id=(to, y), device_id_type=MESH).start()
        return carry

    lax.fori_loop(0, nw - 1, send_b, 0)
    rb[pl.ds(me, 1)] = sb[pl.ds(me, 1)]
    out = pltpu.make_async_copy(gr, grid_hbm, grid_sem)
    out.start()

    basin = iota((nw, BPW), 1).astype(F32)
    for s in range(SLOTS):
        column = im[:, 96 + s:97 + s] * 128.0 + im[:, 112 + s:113 + s]
        one[s * nw:(s + 1) * nw] = jnp.where(column == basin, 1.0, 0.0).astype(BF16)

    pltpu.make_async_copy(sb.at[pl.ds(0, nw - 1)], rb.at[pl.ds(0, nw - 1)], rb_sem).wait()
    val = jnp.transpose(rb[...])
    val = jnp.concatenate([val[s * 4:(s + 1) * 4] for s in range(SLOTS)], axis=1)
    high = val.astype(BF16).astype(F32)
    pair = jnp.concatenate([high, val - high], axis=0).astype(BF16)
    dense = jnp.dot(pair, one[...], preferred_element_type=F32)
    dense = dense[:4] + dense[4:]
    width = BPW // ng
    for g in range(ng):
        sd[g] = dense[:, g * width:(g + 1) * width]
    moves = []
    for k in range(1, ng):
        to = lax.rem(y + k, ng)
        moves.append(pltpu.make_async_remote_copy(
            src_ref=sd.at[to], dst_ref=rd.at[y], send_sem=sd_sem, recv_sem=rd_sem,
            device_id=(me, to), device_id_type=MESH))
        moves[-1].start()
    rd[y] = sd[y]
    pltpu.make_async_copy(sd.at[pl.ds(0, ng - 1)], rd.at[pl.ds(0, ng - 1)], rd_sem).wait()
    sums_ref[...] = rd[...]

    out.wait()
    pltpu.make_async_copy(sa.at[pl.ds(0, nw - 1)], ra.at[pl.ds(0, nw - 1)], sa_sem).wait()
    pltpu.make_async_copy(sb.at[pl.ds(0, nw - 1)], rb.at[pl.ds(0, nw - 1)], sb_sem).wait()
    pltpu.make_async_copy(sd.at[pl.ds(0, ng - 1)], rd.at[pl.ds(0, ng - 1)], sd_sem).wait()


def per_device(spectra, legendre, wave_numbers, block_index, block_weights, basin_index):
    nw, ng = lax.axis_size("wave"), lax.axis_size("basin")
    mloc, ncoef, lats = legendre.shape
    nnz = block_index.shape[1]
    eb = min(128, nnz)
    nq = SLOTS * nw
    width = BPW // ng
    vmem = pl.BlockSpec(memory_space=pltpu.VMEM)
    grid, sums = pl.pallas_call(
        functools.partial(kernel, nw, ng),
        out_shape=(jax.ShapeDtypeStruct((4, 160, 128), BF16),
                   jax.ShapeDtypeStruct((ng, 4, width), F32)),
        in_specs=[vmem, pl.BlockSpec(memory_space=pl.ANY), pl.BlockSpec(memory_space=pltpu.SMEM),
                  vmem, vmem, vmem],
        out_specs=(pl.BlockSpec(memory_space=pl.ANY), vmem),
        scratch_shapes=[
            pltpu.VMEM((mloc, ncoef, lats), BF16),
            pltpu.VMEM((nw, 2, 128), BF16),
            pltpu.VMEM((nw, 2, 128), BF16),
            pltpu.VMEM((nw, 128), F32),
            pltpu.VMEM((nw, 128), F32),
            pltpu.VMEM((ng, 4, width), F32),
            pltpu.VMEM((ng, 4, width), F32),
            pltpu.VMEM((320, 2 * mloc * nw), BF16),
            pltpu.VMEM((2 * mloc * nw, 256), BF16),
            pltpu.VMEM((144, nq), BF16),
            pltpu.VMEM((nq, BPW), BF16),
            pltpu.VMEM((128, nw), F32),
            pltpu.VMEM((4, 160, 128), BF16),
            pltpu.VMEM((nnz, nq), BF16),
            pltpu.SemaphoreType.DMA((mloc,)),
            pltpu.SemaphoreType.DMA,
            pltpu.SemaphoreType.DMA,
            pltpu.SemaphoreType.DMA,
            pltpu.SemaphoreType.DMA,
            pltpu.SemaphoreType.DMA,
            pltpu.SemaphoreType.DMA,
            pltpu.SemaphoreType.DMA,
        ],
        compiler_params=pltpu.CompilerParams(
            collective_id=0, has_side_effects=True, vmem_limit_bytes=40 * 1024 * 1024),
    )(jnp.transpose(spectra, (0, 2, 1, 3)), legendre, wave_numbers,
      block_index.reshape(nnz // eb, eb), block_weights.reshape(nnz, BLOCK),
      basin_index.reshape(nnz // eb, eb))
    grid = jnp.transpose(grid.reshape(4, 80, 2, 128), (0, 2, 1, 3)).reshape(4, 2, 1, NLON)
    return grid, sums.reshape(ng * 4, width)


def solution(mesh):
    in_specs = (
        P("basin", None, "wave", None),
        P("wave", None, None),
        P("wave"),
        P("wave", None),
        P("wave", None, None),
        P("wave", None),
    )
    out_specs = (P("basin", None, "wave", None), P(None, ("wave", "basin")))
    return jax.shard_map(
        per_device, mesh=mesh, in_specs=in_specs, out_specs=out_specs, check_vma=False
    )
```

```python
import functools
import math

import jax
import jax.numpy as jnp
from jax import lax
from jax.experimental import pallas as pl
from jax.experimental.pallas import tpu as pltpu
from jax.sharding import PartitionSpec as P

NLON = 10240
LB = 128
BLOCK = 128
SLOTS = 16
BPW_BITS = 9
BPW = 1 << BPW_BITS
MESH = pl.DeviceIdType.MESH
F32 = jnp.float32
BF16 = jnp.bfloat16

COS_C = [(-1) ** n * math.pi ** (2 * n) / math.factorial(2 * n) for n in range(7)]
SIN_C = [(-1) ** n * math.pi ** (2 * n + 1) / math.factorial(2 * n + 1) for n in range(6)]


def cos_sin(r, turn):
    r = r - turn * jnp.floor(r * (1.0 / turn) + 0.5)
    y = r * (1.0 / turn)
    yy = y * y
    c = jnp.full_like(yy, COS_C[6])
    for k in range(5, -1, -1):
        c = c * yy + COS_C[k]
    s = jnp.full_like(yy, SIN_C[5])
    for k in range(4, -1, -1):
        s = s * yy + SIN_C[k]
    s = s * y
    return 1.0 - 2.0 * (s * s), 2.0 * (s * c)


def each_other(me, nw, act):
    if nw != 128:
        lax.fori_loop(1, nw, lambda k, carry: (act(lax.rem(me + k, nw)), carry)[1], 0)
        return
    x, z, c = me >> 5, (me >> 1) & 15, me & 1
    planes = [(((x + xd) & 3) << 5) | (c ^ cd) for xd in (2, 1, 3, 0) for cd in (1, 0)]

    def level(i, carry):
        there = ((z + 8 + ((i + 1) >> 1) * (2 * (i & 1) - 1)) & 15) << 1
        for plane in planes:
            act(plane | there)
        return carry

    lax.fori_loop(0, 15, level, 0)
    for plane in planes[:-1]:
        act(plane | (z << 1))


def iota(shape, dim):
    return lax.broadcasted_iota(jnp.int32, shape, dim)


def kernel(nw, ng, spec_hbm, leg_hbm, wn_hbm, blk_hbm, wgt_hbm, bas_hbm,
           grid_hbm, sums_ref,
           spec_ref, wn_ref, blk_ref, wgt_ref, bas_ref, leg, sa, ra, sb, rb, sd, rd, tu, ba, ca, sn, ws, one, vs, gr, pm,
           in_sem, leg_sem, grid_sem, sa_sem, ra_sem, sb_sem, rb_sem, sd_sem, rd_sem):
    me, y = lax.axis_index("wave"), lax.axis_index("basin")
    mloc = leg.shape[0]
    nb, eb = bas_ref.shape
    nq = SLOTS * nw

    barrier = pltpu.get_barrier_semaphore()

    def greet(to):
        pl.semaphore_signal(barrier, inc=1, device_id=(to, y), device_id_type=MESH)

    each_other(me, nw, greet)
    for k in range(1, ng):
        pl.semaphore_signal(barrier, inc=1, device_id=(me, lax.rem(y + k, ng)), device_id_type=MESH)

    bring = [pltpu.make_async_copy(*pair, in_sem.at[i]) for i, pair in enumerate((
        (bas_hbm, bas_ref), (spec_hbm, spec_ref), (wn_hbm, wn_ref), (blk_hbm, blk_ref),
        (wgt_hbm, wgt_ref)))]
    for copy in bring[:2]:
        copy.start()
    for m in range(mloc):
        pltpu.make_async_copy(leg_hbm.at[m], leg.at[m], leg_sem.at[m]).start()
    for copy in bring[2:]:
        copy.start()

    bring[0].wait()
    bas = bas_ref[...]
    owner = bas >> BPW_BITS
    local = bas & (BPW - 1)
    upper = (iota((eb, eb), 0) < iota((eb, eb), 1)).astype(F32).astype(BF16)
    owned = [(owner[i:i + 1] == iota((nw, eb), 0)).astype(F32) for i in range(nb)]
    before = jnp.zeros((nw, 1), F32)
    ranks = []
    for i in range(nb):
        inside = jnp.dot(owned[i].astype(BF16), upper, preferred_element_type=F32)
        ranks.append(jnp.sum(owned[i] * (inside + before), axis=0, keepdims=True))
        before = before + jnp.sum(owned[i], axis=1, keepdims=True)
    lane = iota((128, eb), 0)
    where_to = jnp.zeros((nw, 128), F32)
    for i in range(nb):
        high = (local[i:i + 1] >> 7).astype(F32)
        low = (local[i:i + 1] & 127).astype(F32)
        rank = ranks[i].astype(jnp.int32)
        named = jnp.where(lane == rank + 96, high, 0.0) + jnp.where(lane == rank + 112, low, 0.0)
        where_to = where_to + lax.dot_general(
            owned[i].astype(BF16), named.astype(BF16), (((1,), (1,)), ((), ())),
            preferred_element_type=F32)
    rank_rows = jnp.concatenate(ranks, axis=0)
    place = rank_rows * float(nw) + owner.astype(F32)
    place_cols = jnp.transpose(place)

    ncoef = spec_ref.shape[3]
    odd = lax.rem(iota((8, ncoef), 1), 2) == 1
    bring[1].wait()
    sums = []
    for m in range(mloc):
        rows = jnp.concatenate([spec_ref[f, m].astype(F32) for f in range(4)], axis=0)
        both = jnp.concatenate([rows, jnp.where(odd, -rows, rows)], axis=0).astype(BF16)
        pltpu.make_async_copy(leg_hbm.at[m], leg.at[m], leg_sem.at[m]).wait()
        sums.append(jnp.dot(both, leg[m], preferred_element_type=F32))
    sums = jnp.concatenate(sums, axis=0)
    if mloc * 16 % 128:
        sums = jnp.concatenate([sums, jnp.zeros((256 - mloc * 16, nw), F32)], axis=0)
    by_lat = jnp.transpose(sums).astype(BF16)
    src = iota((256, 256), 0)
    dst = iota((256, 256), 1)
    r_of, lane_of = dst >> 7, dst & 127
    m_of, f_of, h_of = lane_of >> 3, (lane_of >> 1) & 3, lane_of & 1
    pick = (src == m_of * 16 + h_of * 8 + f_of * 2 + r_of) & (lane_of < mloc * 8)
    ordered = jnp.dot(by_lat, pick.astype(F32).astype(BF16), preferred_element_type=F32)
    lane = iota((1, 128), 1)
    numbers = jnp.zeros((1, 128), F32)
    bring[2].wait()
    for m in range(mloc):
        wn = wn_ref[m]
        numbers = numbers + jnp.where(lane == 80 + m, (wn >> 7).astype(F32), 0.0)
        numbers = numbers + jnp.where(lane == 96 + m, (wn & 127).astype(F32), 0.0)
    part_re = ordered[:, :128] + numbers
    part_im = ordered[:, 128:] + where_to
    sa[...] = jnp.concatenate([part_re[:, None, :], part_im[:, None, :]], axis=1).astype(BF16)

    pl.semaphore_wait(barrier, nw - 1 + ng - 1)

    def send_a(to):
        pltpu.make_async_remote_copy(
            src_ref=sa.at[pl.ds(to, 1)], dst_ref=ra.at[pl.ds(me, 1)], send_sem=sa_sem,
            recv_sem=ra_sem, device_id=(to, y), device_id_type=MESH).start()

    each_other(me, nw, send_a)
    ra[pl.ds(me, 1)] = sa[pl.ds(me, 1)]

    bring[3].wait()
    bring[4].wait()
    ext = jnp.concatenate(
        [jnp.concatenate([blk_ref[i:i + 1].astype(F32), jnp.zeros((15, eb), F32)], axis=0)
         for i in range(nb)], axis=1)
    turned_w = jnp.concatenate(
        [jnp.transpose(wgt_ref[i * eb:(i + 1) * eb].astype(F32)) for i in range(nb)], axis=1)
    left = jnp.concatenate([turned_w, ext], axis=0).astype(BF16)
    for i in range(nb):
        col = jnp.broadcast_to(place_cols[:, i:i + 1], (eb, 128 if nq >= 128 else nq))
        for c in range(max(1, nq // 128)):
            spot = (iota(col.shape, 1) + c * 128).astype(F32)
            pm[i * eb:(i + 1) * eb, c * 128:c * 128 + col.shape[1]] = jnp.where(
                col == spot, 1.0, 0.0).astype(BF16)
    qc = min(256, nq)
    for c in range(nq // qc):
        ws[:, c * qc:(c + 1) * qc] = jnp.dot(
            left, pm[:, c * qc:(c + 1) * qc], preferred_element_type=F32).astype(BF16)

    a_of = (iota((80, 128), 0) >> 1).astype(F32)
    lane_of = iota((1, 128), 1).astype(F32)
    m_of, b_of = iota((128, LB), 0).astype(F32), iota((128, LB), 1).astype(F32)
    flip = 1.0 - 2.0 * (iota((128, LB), 0) & 1).astype(F32)
    for hi in range(10):
        number = lane_of + 128.0 * hi
        weight = jnp.where(number == 0.0, 1.0, 2.0)
        cos_a, sin_a = cos_sin(number * a_of, 80.0)
        ca[hi], sn[hi] = cos_a * weight, sin_a * weight
        cos_b, sin_b = cos_sin((m_of + 128.0 * hi) * b_of, float(NLON))
        ba[hi * 256:hi * 256 + 128, :128] = cos_b.astype(BF16)
        ba[hi * 256:hi * 256 + 128, 128:] = (cos_b * flip).astype(BF16)
        ba[hi * 256 + 128:hi * 256 + 256, :128] = (-sin_b).astype(BF16)
        ba[hi * 256 + 128:hi * 256 + 256, 128:] = (-sin_b * flip).astype(BF16)

    pltpu.make_async_copy(sa.at[pl.ds(0, nw - 1)], ra.at[pl.ds(0, nw - 1)], ra_sem).wait()

    got = ra[...].astype(F32)
    re, im = got[:, 0, :], got[:, 1, :]
    re_t, im_t = jnp.transpose(re), jnp.transpose(im)
    low_lane = iota((nw, 128), 1).astype(F32)
    lefts, rights = [], []
    for m in range(mloc):
        both = jnp.concatenate([re_t[m * 8:(m + 1) * 8], im_t[m * 8:(m + 1) * 8]], axis=0)
        high = re_t[80 + m:81 + m]
        lefts.append(jnp.concatenate(
            [jnp.where(high == float(hi), both, 0.0) for hi in range(10)], axis=0).astype(BF16))
        rights.append(jnp.where(re[:, 96 + m:97 + m] == low_lane, 1.0, 0.0).astype(BF16))
    columns = jnp.dot(jnp.concatenate(lefts, axis=1), jnp.concatenate(rights, axis=0),
                      preferred_element_type=F32)

    parity = (iota((8, 128), 0) & 1) == 0
    for hi in range(10):
        cos_a, sin_a = ca[hi].reshape(10, 8, 128), sn[hi].reshape(10, 8, 128)
        g_re, g_im = columns[hi * 16:hi * 16 + 8], columns[hi * 16 + 8:hi * 16 + 16]
        for f in range(4):
            fr = jnp.where(parity, g_re[2 * f:2 * f + 1], g_re[2 * f + 1:2 * f + 2])[None]
            fi = jnp.where(parity, g_im[2 * f:2 * f + 1], g_im[2 * f + 1:2 * f + 2])[None]
            t_re = (fr * cos_a - fi * sin_a).reshape(80, 128)
            t_im = (fr * sin_a + fi * cos_a).reshape(80, 128)
            tu[f * 80:(f + 1) * 80, hi * 256:hi * 256 + 128] = t_re.astype(BF16)
            tu[f * 80:(f + 1) * 80, hi * 256 + 128:hi * 256 + 256] = t_im.astype(BF16)
    scale = 1.0 / math.sqrt(2.0 * mloc * nw)
    lines = jnp.dot(tu[...], ba[...], preferred_element_type=F32) * scale
    for f in range(4):
        gr[f, :80] = lines[f * 80:(f + 1) * 80, :128].astype(BF16)
        gr[f, 80:] = lines[f * 80:(f + 1) * 80, 128:].astype(BF16)

    row = iota((160, qc), 0)
    block_of = (row & 1) * 80 + (row >> 1)
    block_of = block_of.astype(F32)
    for c in range(nq // qc):
        cols = slice(c * qc, (c + 1) * qc)
        hit = block_of == ws[128:129, cols].astype(F32)
        prod = jnp.dot(gr[...].reshape(640, 128), ws[:128, cols], preferred_element_type=F32)
        val = jnp.concatenate(
            [jnp.sum(jnp.where(hit, prod[f * 160:(f + 1) * 160], 0.0), axis=0, keepdims=True)
             for f in range(4)], axis=0)
        high = val.astype(BF16).astype(F32)
        val = jnp.concatenate([high, val - high], axis=0)
        for j in range(qc // nw):
            s = c * (qc // nw) + j
            vs[s * 8:(s + 1) * 8] = val[:, j * nw:(j + 1) * nw]
    sb[...] = jnp.transpose(vs[...])

    def send_b(to):
        pltpu.make_async_remote_copy(
            src_ref=sb.at[pl.ds(to, 1)], dst_ref=rb.at[pl.ds(me, 1)], send_sem=sb_sem,
            recv_sem=rb_sem, device_id=(to, y), device_id_type=MESH).start()

    each_other(me, nw, send_b)
    rb[pl.ds(me, 1)] = sb[pl.ds(me, 1)]
    out = pltpu.make_async_copy(gr, grid_hbm, grid_sem)
    out.start()

    for s in range(SLOTS):
        one[s * nw:(s + 1) * nw] = jnp.where(
            im[:, 112 + s:113 + s] == low_lane, 1.0, 0.0).astype(BF16)

    pltpu.make_async_copy(sb.at[pl.ds(0, nw - 1)], rb.at[pl.ds(0, nw - 1)], rb_sem).wait()
    val = jnp.transpose(rb[...])
    named = []
    for s in range(SLOTS):
        high = im_t[96 + s:97 + s]
        named.append(jnp.concatenate(
            [jnp.where(high == float(hi), val[s * 8:(s + 1) * 8], 0.0) for hi in range(BPW // 128)],
            axis=0).astype(BF16))
    dense = jnp.dot(jnp.concatenate(named, axis=1), one[...], preferred_element_type=F32)
    dense = [dense[hi * 8:hi * 8 + 4] + dense[hi * 8 + 4:hi * 8 + 8] for hi in range(BPW // 128)]
    each = BPW // 128 // ng
    for g in range(ng):
        for k in range(each):
            sd[g, :, k * 128:(k + 1) * 128] = dense[g * each + k]
    moves = []
    for k in range(1, ng):
        to = lax.rem(y + k, ng)
        moves.append(pltpu.make_async_remote_copy(
            src_ref=sd.at[to], dst_ref=rd.at[y], send_sem=sd_sem, recv_sem=rd_sem,
            device_id=(me, to), device_id_type=MESH))
        moves[-1].start()
    rd[y] = sd[y]
    pltpu.make_async_copy(sd.at[pl.ds(0, ng - 1)], rd.at[pl.ds(0, ng - 1)], rd_sem).wait()
    sums_ref[...] = rd[...]

    out.wait()
    pltpu.make_async_copy(sa.at[pl.ds(0, nw - 1)], ra.at[pl.ds(0, nw - 1)], sa_sem).wait()
    pltpu.make_async_copy(sb.at[pl.ds(0, nw - 1)], rb.at[pl.ds(0, nw - 1)], sb_sem).wait()
    pltpu.make_async_copy(sd.at[pl.ds(0, ng - 1)], rd.at[pl.ds(0, ng - 1)], sd_sem).wait()


def per_device(spectra, legendre, wave_numbers, block_index, block_weights, basin_index):
    nw, ng = lax.axis_size("wave"), lax.axis_size("basin")
    mloc, ncoef, lats = legendre.shape
    nnz = block_index.shape[1]
    eb = min(128, nnz)
    nq = SLOTS * nw
    width = BPW // ng
    vmem = pl.BlockSpec(memory_space=pltpu.VMEM)
    grid, sums = pl.pallas_call(
        functools.partial(kernel, nw, ng),
        out_shape=(jax.ShapeDtypeStruct((4, 160, 128), BF16),
                   jax.ShapeDtypeStruct((ng, 4, width), F32)),
        in_specs=[pl.BlockSpec(memory_space=pltpu.HBM)] * 6,
        out_specs=(pl.BlockSpec(memory_space=pl.ANY), vmem),
        scratch_shapes=[
            pltpu.VMEM((4, mloc, 2, ncoef), BF16),
            pltpu.SMEM((mloc,), jnp.int32),
            pltpu.VMEM((nnz // eb, eb), jnp.int32),
            pltpu.VMEM((nnz, BLOCK), BF16),
            pltpu.VMEM((nnz // eb, eb), jnp.int32),
            pltpu.VMEM((mloc, ncoef, lats), BF16),
            pltpu.VMEM((nw, 2, 128), BF16),
            pltpu.VMEM((nw, 2, 128), BF16),
            pltpu.VMEM((nw, 128), F32),
            pltpu.VMEM((nw, 128), F32),
            pltpu.VMEM((ng, 4, width), F32),
            pltpu.VMEM((ng, 4, width), F32),
            pltpu.VMEM((320, 2560), BF16),
            pltpu.VMEM((2560, 256), BF16),
            pltpu.VMEM((10, 80, 128), F32),
            pltpu.VMEM((10, 80, 128), F32),
            pltpu.VMEM((144, nq), BF16),
            pltpu.VMEM((nq, 128), BF16),
            pltpu.VMEM((128, nw), F32),
            pltpu.VMEM((4, 160, 128), BF16),
            pltpu.VMEM((nnz, nq), BF16),
            pltpu.SemaphoreType.DMA((5,)),
            pltpu.SemaphoreType.DMA((mloc,)),
            pltpu.SemaphoreType.DMA,
            pltpu.SemaphoreType.DMA,
            pltpu.SemaphoreType.DMA,
            pltpu.SemaphoreType.DMA,
            pltpu.SemaphoreType.DMA,
            pltpu.SemaphoreType.DMA,
            pltpu.SemaphoreType.DMA,
        ],
        compiler_params=pltpu.CompilerParams(
            collective_id=0, has_side_effects=True, vmem_limit_bytes=40 * 1024 * 1024),
    )(*[pltpu.with_memory_space_constraint(x, pltpu.HBM) for x in (
        jnp.transpose(spectra, (0, 2, 1, 3)), legendre, wave_numbers,
        block_index.reshape(nnz // eb, eb), block_weights.reshape(nnz, BLOCK),
        basin_index.reshape(nnz // eb, eb))])
    grid = jnp.transpose(grid.reshape(4, 80, 2, 128), (0, 2, 1, 3)).reshape(4, 2, 1, NLON)
    return grid, sums.reshape(ng * 4, width)


def solution(mesh):
    in_specs = (
        P("basin", None, "wave", None),
        P("wave", None, None),
        P("wave"),
        P("wave", None),
        P("wave", None, None),
        P("wave", None),
    )
    out_specs = (P("basin", None, "wave", None), P(None, ("wave", "basin")))
    return jax.shard_map(
        per_device, mesh=mesh, in_specs=in_specs, out_specs=out_specs, check_vma=False
    )
```

```python
import functools
import math

import jax
import jax.numpy as jnp
from jax import lax
from jax.experimental import pallas as pl
from jax.experimental.pallas import tpu as pltpu
from jax.sharding import PartitionSpec as P

NLON = 10240
LB = 128
BLOCK = 128
SLOTS = 16
BPW_BITS = 9
BPW = 1 << BPW_BITS
MESH = pl.DeviceIdType.MESH
F32 = jnp.float32
BF16 = jnp.bfloat16

COS_C = [(-1) ** n * math.pi ** (2 * n) / math.factorial(2 * n) for n in range(7)]
SIN_C = [(-1) ** n * math.pi ** (2 * n + 1) / math.factorial(2 * n + 1) for n in range(6)]


def cos_sin(r, turn):
    r = r - turn * jnp.floor(r * (1.0 / turn) + 0.5)
    y = r * (1.0 / turn)
    yy = y * y
    c = jnp.full_like(yy, COS_C[6])
    for k in range(5, -1, -1):
        c = c * yy + COS_C[k]
    s = jnp.full_like(yy, SIN_C[5])
    for k in range(4, -1, -1):
        s = s * yy + SIN_C[k]
    s = s * y
    return 1.0 - 2.0 * (s * s), 2.0 * (s * c)


def each_other(me, nw, act):
    if nw != 128:
        lax.fori_loop(1, nw, lambda k, carry: (act(lax.rem(me + k, nw)), carry)[1], 0)
        return
    x, z, c = me >> 5, (me >> 1) & 15, me & 1
    planes = [(((x + xd) & 3) << 5) | (c ^ cd) for xd in (2, 1, 3, 0) for cd in (1, 0)]

    def level(i, carry):
        there = ((z + 8 + ((i + 1) >> 1) * (2 * (i & 1) - 1)) & 15) << 1
        for plane in planes:
            act(plane | there)
        return carry

    lax.fori_loop(0, 15, level, 0)
    for plane in planes[:-1]:
        act(plane | (z << 1))


def iota(shape, dim):
    return lax.broadcasted_iota(jnp.int32, shape, dim)


def kernel(nw, ng, spec_hbm, leg_hbm, wn_hbm, blk_hbm, wgt_hbm, bas_hbm,
           grid_hbm, sums_ref,
           spec_ref, wn_ref, blk_ref, wgt_ref, bas_ref, leg, sa, ra, rz, sb, rb, sd, rd, tu, ba, ca, sn, ws, one, vs, gr, pm,
           in_sem, leg_sem, grid_sem, sa_sem, ra_sem, sz_sem, rz_sem, sb_sem, rb_sem, sd_sem, rd_sem):
    me, y = lax.axis_index("wave"), lax.axis_index("basin")
    mloc = leg.shape[0]
    nb, eb = bas_ref.shape
    nq = SLOTS * nw

    barrier = pltpu.get_barrier_semaphore()

    def greet(to):
        pl.semaphore_signal(barrier, inc=1, device_id=(to, y), device_id_type=MESH)

    @pl.when(me != 0)
    def _():
        each_other(me, nw, greet)

    @pl.when(me == 0)
    def _():
        greet(1)

    for k in range(1, ng):
        pl.semaphore_signal(barrier, inc=1, device_id=(me, lax.rem(y + k, ng)), device_id_type=MESH)

    bring = [pltpu.make_async_copy(*pair, in_sem.at[i]) for i, pair in enumerate((
        (bas_hbm, bas_ref), (spec_hbm, spec_ref), (wn_hbm, wn_ref), (blk_hbm, blk_ref),
        (wgt_hbm, wgt_ref)))]
    for copy in bring[:2]:
        copy.start()
    for m in range(mloc):
        pltpu.make_async_copy(leg_hbm.at[m], leg.at[m], leg_sem.at[m]).start()
    for copy in bring[2:]:
        copy.start()

    bring[0].wait()
    bas = bas_ref[...]
    owner = bas >> BPW_BITS
    local = bas & (BPW - 1)
    upper = (iota((eb, eb), 0) < iota((eb, eb), 1)).astype(F32).astype(BF16)
    owned = [(owner[i:i + 1] == iota((nw, eb), 0)).astype(F32) for i in range(nb)]
    before = jnp.zeros((nw, 1), F32)
    ranks = []
    for i in range(nb):
        inside = jnp.dot(owned[i].astype(BF16), upper, preferred_element_type=F32)
        ranks.append(jnp.sum(owned[i] * (inside + before), axis=0, keepdims=True))
        before = before + jnp.sum(owned[i], axis=1, keepdims=True)
    lane = iota((128, eb), 0)
    where_to = jnp.zeros((nw, 128), F32)
    for i in range(nb):
        high = (local[i:i + 1] >> 7).astype(F32)
        low = (local[i:i + 1] & 127).astype(F32)
        rank = ranks[i].astype(jnp.int32)
        named = jnp.where(lane == rank + 96, high, 0.0) + jnp.where(lane == rank + 112, low, 0.0)
        where_to = where_to + lax.dot_general(
            owned[i].astype(BF16), named.astype(BF16), (((1,), (1,)), ((), ())),
            preferred_element_type=F32)
    rank_rows = jnp.concatenate(ranks, axis=0)
    place = rank_rows * float(nw) + owner.astype(F32)
    place_cols = jnp.transpose(place)

    ncoef = spec_ref.shape[3]
    odd = lax.rem(iota((8, ncoef), 1), 2) == 1
    bring[1].wait()
    sums = []
    for m in range(mloc):
        rows = jnp.concatenate([spec_ref[f, m].astype(F32) for f in range(4)], axis=0)
        both = jnp.concatenate([rows, jnp.where(odd, -rows, rows)], axis=0).astype(BF16)
        pltpu.make_async_copy(leg_hbm.at[m], leg.at[m], leg_sem.at[m]).wait()
        sums.append(jnp.dot(both, leg[m], preferred_element_type=F32))
    sums = jnp.concatenate(sums, axis=0)
    if mloc * 16 % 128:
        sums = jnp.concatenate([sums, jnp.zeros((256 - mloc * 16, nw), F32)], axis=0)
    by_lat = jnp.transpose(sums).astype(BF16)
    src = iota((256, 256), 0)
    dst = iota((256, 256), 1)
    r_of, lane_of = dst >> 7, dst & 127
    m_of, f_of, h_of = lane_of >> 3, (lane_of >> 1) & 3, lane_of & 1
    pick = (src == m_of * 16 + h_of * 8 + f_of * 2 + r_of) & (lane_of < mloc * 8)
    ordered = jnp.dot(by_lat, pick.astype(F32).astype(BF16), preferred_element_type=F32)
    lane = iota((1, 128), 1)
    numbers = jnp.zeros((1, 128), F32)
    bring[2].wait()
    for m in range(mloc):
        wn = wn_ref[m]
        numbers = numbers + jnp.where(lane == 80 + m, (wn >> 7).astype(F32), 0.0)
        numbers = numbers + jnp.where(lane == 96 + m, (wn & 127).astype(F32), 0.0)
    part_re = ordered[:, :128] + numbers
    part_im = ordered[:, 128:] + where_to
    sa[...] = jnp.concatenate([part_re[:, None, :], part_im[:, None, :]], axis=1).astype(BF16)

    pl.semaphore_wait(barrier, nw - 1 + ng - 1 - (me > 1).astype(jnp.int32))

    @pl.when(me > 1)
    def _():
        pltpu.make_async_remote_copy(
            src_ref=sa.at[pl.ds(0, 1)], dst_ref=rz.at[pl.ds(me, 1)], send_sem=sz_sem,
            recv_sem=rz_sem, device_id=(1, y), device_id_type=MESH).start()

    def send_a(to):
        @pl.when(to != 0)
        def _():
            pltpu.make_async_remote_copy(
                src_ref=sa.at[pl.ds(to, 1)], dst_ref=ra.at[pl.ds(me, 1)], send_sem=sa_sem,
                recv_sem=ra_sem, device_id=(to, y), device_id_type=MESH).start()

    each_other(me, nw, send_a)
    ra[pl.ds(me, 1)] = sa[pl.ds(me, 1)]

    bring[3].wait()
    bring[4].wait()
    ext = jnp.concatenate(
        [jnp.concatenate([blk_ref[i:i + 1].astype(F32), jnp.zeros((15, eb), F32)], axis=0)
         for i in range(nb)], axis=1)
    turned_w = jnp.concatenate(
        [jnp.transpose(wgt_ref[i * eb:(i + 1) * eb].astype(F32)) for i in range(nb)], axis=1)
    left = jnp.concatenate([turned_w, ext], axis=0).astype(BF16)
    for i in range(nb):
        col = jnp.broadcast_to(place_cols[:, i:i + 1], (eb, 128 if nq >= 128 else nq))
        for c in range(max(1, nq // 128)):
            spot = (iota(col.shape, 1) + c * 128).astype(F32)
            pm[i * eb:(i + 1) * eb, c * 128:c * 128 + col.shape[1]] = jnp.where(
                col == spot, 1.0, 0.0).astype(BF16)
    qc = min(256, nq)
    for c in range(nq // qc):
        ws[:, c * qc:(c + 1) * qc] = jnp.dot(
            left, pm[:, c * qc:(c + 1) * qc], preferred_element_type=F32).astype(BF16)

    a_of = (iota((80, 128), 0) >> 1).astype(F32)
    lane_of = iota((1, 128), 1).astype(F32)
    m_of, b_of = iota((128, LB), 0).astype(F32), iota((128, LB), 1).astype(F32)
    flip = 1.0 - 2.0 * (iota((128, LB), 0) & 1).astype(F32)
    for hi in range(10):
        number = lane_of + 128.0 * hi
        weight = jnp.where(number == 0.0, 1.0, 2.0)
        cos_a, sin_a = cos_sin(number * a_of, 80.0)
        ca[hi], sn[hi] = cos_a * weight, sin_a * weight
        cos_b, sin_b = cos_sin((m_of + 128.0 * hi) * b_of, float(NLON))
        ba[hi * 256:hi * 256 + 128, :128] = cos_b.astype(BF16)
        ba[hi * 256:hi * 256 + 128, 128:] = (cos_b * flip).astype(BF16)
        ba[hi * 256 + 128:hi * 256 + 256, :128] = (-sin_b).astype(BF16)
        ba[hi * 256 + 128:hi * 256 + 256, 128:] = (-sin_b * flip).astype(BF16)

    pass_on = pltpu.make_async_remote_copy(
        src_ref=rz.at[pl.ds(1, nw - 1)], dst_ref=ra.at[pl.ds(1, nw - 1)], send_sem=sz_sem,
        recv_sem=ra_sem, device_id=(0, y), device_id_type=MESH)

    @pl.when(me == 1)
    def _():
        rz[1] = sa[0]
        pltpu.make_async_copy(sa.at[pl.ds(0, nw - 2)], rz.at[pl.ds(0, nw - 2)], rz_sem).wait()
        pass_on.start()

    pltpu.make_async_copy(sa.at[pl.ds(0, nw - 1)], ra.at[pl.ds(0, nw - 1)], ra_sem).wait()

    got = ra[...].astype(F32)
    re, im = got[:, 0, :], got[:, 1, :]
    re_t, im_t = jnp.transpose(re), jnp.transpose(im)
    low_lane = iota((nw, 128), 1).astype(F32)
    lefts, rights = [], []
    for m in range(mloc):
        both = jnp.concatenate([re_t[m * 8:(m + 1) * 8], im_t[m * 8:(m + 1) * 8]], axis=0)
        high = re_t[80 + m:81 + m]
        lefts.append(jnp.concatenate(
            [jnp.where(high == float(hi), both, 0.0) for hi in range(10)], axis=0).astype(BF16))
        rights.append(jnp.where(re[:, 96 + m:97 + m] == low_lane, 1.0, 0.0).astype(BF16))
    columns = jnp.dot(jnp.concatenate(lefts, axis=1), jnp.concatenate(rights, axis=0),
                      preferred_element_type=F32)

    parity = (iota((8, 128), 0) & 1) == 0
    for hi in range(10):
        cos_a, sin_a = ca[hi].reshape(10, 8, 128), sn[hi].reshape(10, 8, 128)
        g_re, g_im = columns[hi * 16:hi * 16 + 8], columns[hi * 16 + 8:hi * 16 + 16]
        for f in range(4):
            fr = jnp.where(parity, g_re[2 * f:2 * f + 1], g_re[2 * f + 1:2 * f + 2])[None]
            fi = jnp.where(parity, g_im[2 * f:2 * f + 1], g_im[2 * f + 1:2 * f + 2])[None]
            t_re = (fr * cos_a - fi * sin_a).reshape(80, 128)
            t_im = (fr * sin_a + fi * cos_a).reshape(80, 128)
            tu[f * 80:(f + 1) * 80, hi * 256:hi * 256 + 128] = t_re.astype(BF16)
            tu[f * 80:(f + 1) * 80, hi * 256 + 128:hi * 256 + 256] = t_im.astype(BF16)
    scale = 1.0 / math.sqrt(2.0 * mloc * nw)
    lines = jnp.dot(tu[...], ba[...], preferred_element_type=F32) * scale
    for f in range(4):
        gr[f, :80] = lines[f * 80:(f + 1) * 80, :128].astype(BF16)
        gr[f, 80:] = lines[f * 80:(f + 1) * 80, 128:].astype(BF16)

    row = iota((160, qc), 0)
    block_of = (row & 1) * 80 + (row >> 1)
    block_of = block_of.astype(F32)
    for c in range(nq // qc):
        cols = slice(c * qc, (c + 1) * qc)
        hit = block_of == ws[128:129, cols].astype(F32)
        prod = jnp.dot(gr[...].reshape(640, 128), ws[:128, cols], preferred_element_type=F32)
        val = jnp.concatenate(
            [jnp.sum(jnp.where(hit, prod[f * 160:(f + 1) * 160], 0.0), axis=0, keepdims=True)
             for f in range(4)], axis=0)
        high = val.astype(BF16).astype(F32)
        val = jnp.concatenate([high, val - high], axis=0)
        for j in range(qc // nw):
            s = c * (qc // nw) + j
            vs[s * 8:(s + 1) * 8] = val[:, j * nw:(j + 1) * nw]
    sb[...] = jnp.transpose(vs[...])

    def send_b(to):
        pltpu.make_async_remote_copy(
            src_ref=sb.at[pl.ds(to, 1)], dst_ref=rb.at[pl.ds(me, 1)], send_sem=sb_sem,
            recv_sem=rb_sem, device_id=(to, y), device_id_type=MESH).start()

    each_other(me, nw, send_b)
    rb[pl.ds(me, 1)] = sb[pl.ds(me, 1)]
    out = pltpu.make_async_copy(gr, grid_hbm, grid_sem)
    out.start()

    for s in range(SLOTS):
        one[s * nw:(s + 1) * nw] = jnp.where(
            im[:, 112 + s:113 + s] == low_lane, 1.0, 0.0).astype(BF16)

    pltpu.make_async_copy(sb.at[pl.ds(0, nw - 1)], rb.at[pl.ds(0, nw - 1)], rb_sem).wait()
    val = jnp.transpose(rb[...])
    named = []
    for s in range(SLOTS):
        high = im_t[96 + s:97 + s]
        named.append(jnp.concatenate(
            [jnp.where(high == float(hi), val[s * 8:(s + 1) * 8], 0.0) for hi in range(BPW // 128)],
            axis=0).astype(BF16))
    dense = jnp.dot(jnp.concatenate(named, axis=1), one[...], preferred_element_type=F32)
    dense = [dense[hi * 8:hi * 8 + 4] + dense[hi * 8 + 4:hi * 8 + 8] for hi in range(BPW // 128)]
    each = BPW // 128 // ng
    for g in range(ng):
        for k in range(each):
            sd[g, :, k * 128:(k + 1) * 128] = dense[g * each + k]
    moves = []
    for k in range(1, ng):
        to = lax.rem(y + k, ng)
        moves.append(pltpu.make_async_remote_copy(
            src_ref=sd.at[to], dst_ref=rd.at[y], send_sem=sd_sem, recv_sem=rd_sem,
            device_id=(me, to), device_id_type=MESH))
        moves[-1].start()
    rd[y] = sd[y]
    pltpu.make_async_copy(sd.at[pl.ds(0, ng - 1)], rd.at[pl.ds(0, ng - 1)], rd_sem).wait()
    sums_ref[...] = rd[...]

    out.wait()
    @pl.when(me == 0)
    def _():
        pltpu.make_async_copy(sa.at[pl.ds(0, nw - 1)], ra.at[pl.ds(0, nw - 1)], sa_sem).wait()

    @pl.when(me != 0)
    def _():
        pltpu.make_async_copy(sa.at[pl.ds(0, nw - 2)], ra.at[pl.ds(0, nw - 2)], sa_sem).wait()

    @pl.when(me == 1)
    def _():
        pass_on.wait_send()

    @pl.when(me > 1)
    def _():
        pltpu.make_async_copy(sa.at[pl.ds(0, 1)], rz.at[pl.ds(0, 1)], sz_sem).wait()

    pltpu.make_async_copy(sb.at[pl.ds(0, nw - 1)], rb.at[pl.ds(0, nw - 1)], sb_sem).wait()
    pltpu.make_async_copy(sd.at[pl.ds(0, ng - 1)], rd.at[pl.ds(0, ng - 1)], sd_sem).wait()


def per_device(spectra, legendre, wave_numbers, block_index, block_weights, basin_index):
    nw, ng = lax.axis_size("wave"), lax.axis_size("basin")
    mloc, ncoef, lats = legendre.shape
    nnz = block_index.shape[1]
    eb = min(128, nnz)
    nq = SLOTS * nw
    width = BPW // ng
    vmem = pl.BlockSpec(memory_space=pltpu.VMEM)
    grid, sums = pl.pallas_call(
        functools.partial(kernel, nw, ng),
        out_shape=(jax.ShapeDtypeStruct((4, 160, 128), BF16),
                   jax.ShapeDtypeStruct((ng, 4, width), F32)),
        in_specs=[pl.BlockSpec(memory_space=pltpu.HBM)] * 6,
        out_specs=(pl.BlockSpec(memory_space=pl.ANY), vmem),
        scratch_shapes=[
            pltpu.VMEM((4, mloc, 2, ncoef), BF16),
            pltpu.SMEM((mloc,), jnp.int32),
            pltpu.VMEM((nnz // eb, eb), jnp.int32),
            pltpu.VMEM((nnz, BLOCK), BF16),
            pltpu.VMEM((nnz // eb, eb), jnp.int32),
            pltpu.VMEM((mloc, ncoef, lats), BF16),
            pltpu.VMEM((nw, 2, 128), BF16),
            pltpu.VMEM((nw, 2, 128), BF16),
            pltpu.VMEM((nw, 2, 128), BF16),
            pltpu.VMEM((nw, 128), F32),
            pltpu.VMEM((nw, 128), F32),
            pltpu.VMEM((ng, 4, width), F32),
            pltpu.VMEM((ng, 4, width), F32),
            pltpu.VMEM((320, 2560), BF16),
            pltpu.VMEM((2560, 256), BF16),
            pltpu.VMEM((10, 80, 128), F32),
            pltpu.VMEM((10, 80, 128), F32),
            pltpu.VMEM((144, nq), BF16),
            pltpu.VMEM((nq, 128), BF16),
            pltpu.VMEM((128, nw), F32),
            pltpu.VMEM((4, 160, 128), BF16),
            pltpu.VMEM((nnz, nq), BF16),
            pltpu.SemaphoreType.DMA((5,)),
            pltpu.SemaphoreType.DMA((mloc,)),
            pltpu.SemaphoreType.DMA,
            pltpu.SemaphoreType.DMA,
            pltpu.SemaphoreType.DMA,
            pltpu.SemaphoreType.DMA,
            pltpu.SemaphoreType.DMA,
            pltpu.SemaphoreType.DMA,
            pltpu.SemaphoreType.DMA,
            pltpu.SemaphoreType.DMA,
            pltpu.SemaphoreType.DMA,
        ],
        compiler_params=pltpu.CompilerParams(
            collective_id=0, has_side_effects=True, vmem_limit_bytes=40 * 1024 * 1024),
    )(*[pltpu.with_memory_space_constraint(x, pltpu.HBM) for x in (
        jnp.transpose(spectra, (0, 2, 1, 3)), legendre, wave_numbers,
        block_index.reshape(nnz // eb, eb), block_weights.reshape(nnz, BLOCK),
        basin_index.reshape(nnz // eb, eb))])
    grid = jnp.transpose(grid.reshape(4, 80, 2, 128), (0, 2, 1, 3)).reshape(4, 2, 1, NLON)
    return grid, sums.reshape(ng * 4, width)


def solution(mesh):
    in_specs = (
        P("basin", None, "wave", None),
        P("wave", None, None),
        P("wave"),
        P("wave", None),
        P("wave", None, None),
        P("wave", None),
    )
    out_specs = (P("basin", None, "wave", None), P(None, ("wave", "basin")))
    return jax.shard_map(
        per_device, mesh=mesh, in_specs=in_specs, out_specs=out_specs, check_vma=False
    )
```

```python
import functools
import math

import jax
import jax.numpy as jnp
from jax import lax
from jax.experimental import pallas as pl
from jax.experimental.pallas import tpu as pltpu
from jax.sharding import PartitionSpec as P

NLON = 10240
LB = 128
BLOCK = 128
SLOTS = 16
BPW_BITS = 9
BPW = 1 << BPW_BITS
MESH = pl.DeviceIdType.MESH
F32 = jnp.float32
BF16 = jnp.bfloat16

COS_C = [(-1) ** n * math.pi ** (2 * n) / math.factorial(2 * n) for n in range(7)]
SIN_C = [(-1) ** n * math.pi ** (2 * n + 1) / math.factorial(2 * n + 1) for n in range(6)]


def cos_sin(r, turn):
    r = r - turn * jnp.floor(r * (1.0 / turn) + 0.5)
    y = r * (1.0 / turn)
    yy = y * y
    c = jnp.full_like(yy, COS_C[6])
    for k in range(5, -1, -1):
        c = c * yy + COS_C[k]
    s = jnp.full_like(yy, SIN_C[5])
    for k in range(4, -1, -1):
        s = s * yy + SIN_C[k]
    s = s * y
    return 1.0 - 2.0 * (s * s), 2.0 * (s * c)


def each_other(me, nw, act):
    if nw != 128:
        lax.fori_loop(1, nw, lambda k, carry: (act(lax.rem(me + k, nw)), carry)[1], 0)
        return
    x, z, c = me >> 5, (me >> 1) & 15, me & 1
    planes = [(((x + xd) & 3) << 5) | (c ^ cd) for xd in (2, 1, 3, 0) for cd in (1, 0)]

    def level(i, carry):
        there = ((z + 8 + ((i + 1) >> 1) * (2 * (i & 1) - 1)) & 15) << 1
        for plane in planes:
            act(plane | there)
        return carry

    lax.fori_loop(0, 15, level, 0)
    for plane in planes[:-1]:
        act(plane | (z << 1))


def iota(shape, dim):
    return lax.broadcasted_iota(jnp.int32, shape, dim)


def kernel(nw, ng, spec_hbm, leg_hbm, wn_hbm, blk_hbm, wgt_hbm, bas_hbm,
           grid_hbm, sums_ref,
           spec_ref, wn_ref, blk_ref, wgt_ref, bas_ref, leg, sa, ra, sb, rb, sd, rd, tu, ba, ca, sn, ws, key, one, vs, gr, pm,
           in_sem, leg_sem, grid_sem, sa_sem, ra_sem, sb_sem, rb_sem, sd_sem, rd_sem):
    me, y = lax.axis_index("wave"), lax.axis_index("basin")
    mloc = leg.shape[0]
    nb, eb = bas_ref.shape
    nq = SLOTS * nw

    barrier = pltpu.get_barrier_semaphore()

    def greet(to):
        pl.semaphore_signal(barrier, inc=1, device_id=(to, y), device_id_type=MESH)

    each_other(me, nw, greet)
    for k in range(1, ng):
        pl.semaphore_signal(barrier, inc=1, device_id=(me, lax.rem(y + k, ng)), device_id_type=MESH)

    bring = [pltpu.make_async_copy(*pair, in_sem.at[i]) for i, pair in enumerate((
        (bas_hbm, bas_ref), (spec_hbm, spec_ref), (wn_hbm, wn_ref), (blk_hbm, blk_ref),
        (wgt_hbm, wgt_ref)))]
    for copy in bring[:2]:
        copy.start()
    for m in range(mloc):
        pltpu.make_async_copy(leg_hbm.at[m], leg.at[m], leg_sem.at[m]).start()
    for copy in bring[2:]:
        copy.start()

    bring[0].wait()
    bas = bas_ref[...]
    owner = bas >> BPW_BITS
    local = bas & (BPW - 1)
    upper = (iota((eb, eb), 0) < iota((eb, eb), 1)).astype(F32).astype(BF16)
    owned = [(owner[i:i + 1] == iota((nw, eb), 0)).astype(F32) for i in range(nb)]
    before = jnp.zeros((nw, 1), F32)
    ranks = []
    for i in range(nb):
        inside = jnp.dot(owned[i].astype(BF16), upper, preferred_element_type=F32)
        ranks.append(jnp.sum(owned[i] * (inside + before), axis=0, keepdims=True))
        before = before + jnp.sum(owned[i], axis=1, keepdims=True)
    lane = iota((128, eb), 0)
    where_to = jnp.zeros((nw, 128), F32)
    for i in range(nb):
        high = (local[i:i + 1] >> 7).astype(F32)
        low = (local[i:i + 1] & 127).astype(F32)
        rank = ranks[i].astype(jnp.int32)
        named = jnp.where(lane == rank + 96, high, 0.0) + jnp.where(lane == rank + 112, low, 0.0)
        where_to = where_to + lax.dot_general(
            owned[i].astype(BF16), named.astype(BF16), (((1,), (1,)), ((), ())),
            preferred_element_type=F32)
    rank_rows = jnp.concatenate(ranks, axis=0)
    place = rank_rows * float(nw) + owner.astype(F32)
    place_cols = jnp.transpose(place)

    ncoef = spec_ref.shape[3]
    odd = lax.rem(iota((8, ncoef), 1), 2) == 1
    bring[1].wait()
    sums = []
    for m in range(mloc):
        rows = jnp.concatenate([spec_ref[f, m].astype(F32) for f in range(4)], axis=0)
        both = jnp.concatenate([rows, jnp.where(odd, -rows, rows)], axis=0).astype(BF16)
        pltpu.make_async_copy(leg_hbm.at[m], leg.at[m], leg_sem.at[m]).wait()
        sums.append(jnp.dot(both, leg[m], preferred_element_type=F32))
    sums = jnp.concatenate(sums, axis=0)
    if mloc * 16 % 128:
        sums = jnp.concatenate([sums, jnp.zeros((256 - mloc * 16, nw), F32)], axis=0)
    by_lat = jnp.transpose(sums).astype(BF16)
    src = iota((256, 256), 0)
    dst = iota((256, 256), 1)
    r_of, lane_of = dst >> 7, dst & 127
    m_of, f_of, h_of = lane_of >> 3, (lane_of >> 1) & 3, lane_of & 1
    pick = (src == m_of * 16 + h_of * 8 + f_of * 2 + r_of) & (lane_of < mloc * 8)
    ordered = jnp.dot(by_lat, pick.astype(F32).astype(BF16), preferred_element_type=F32)
    lane = iota((1, 128), 1)
    numbers = jnp.zeros((1, 128), F32)
    bring[2].wait()
    for m in range(mloc):
        wn = wn_ref[m]
        chunk = (wn & 1) * 5 + (wn >> 8)
        numbers = numbers + jnp.where(lane == 80 + m, chunk.astype(F32), 0.0)
        numbers = numbers + jnp.where(lane == 96 + m, ((wn >> 1) & 127).astype(F32), 0.0)
    part_re = ordered[:, :128] + numbers
    part_im = ordered[:, 128:] + where_to
    sa[...] = jnp.concatenate([part_re[:, None, :], part_im[:, None, :]], axis=1).astype(BF16)

    pl.semaphore_wait(barrier, nw - 1 + ng - 1)

    def send_a(to):
        pltpu.make_async_remote_copy(
            src_ref=sa.at[pl.ds(to, 1)], dst_ref=ra.at[pl.ds(me, 1)], send_sem=sa_sem,
            recv_sem=ra_sem, device_id=(to, y), device_id_type=MESH).start()

    each_other(me, nw, send_a)
    ra[pl.ds(me, 1)] = sa[pl.ds(me, 1)]

    bring[3].wait()
    bring[4].wait()
    ext = jnp.concatenate(
        [jnp.concatenate([blk_ref[i:i + 1].astype(F32), jnp.zeros((15, eb), F32)], axis=0)
         for i in range(nb)], axis=1)
    turned_w = jnp.concatenate(
        [jnp.transpose(wgt_ref[i * eb:(i + 1) * eb].astype(F32)) for i in range(nb)], axis=1)
    left = jnp.concatenate([turned_w, ext], axis=0).astype(BF16)
    for i in range(nb):
        col = jnp.broadcast_to(place_cols[:, i:i + 1], (eb, 128 if nq >= 128 else nq))
        for c in range(max(1, nq // 128)):
            spot = (iota(col.shape, 1) + c * 128).astype(F32)
            pm[i * eb:(i + 1) * eb, c * 128:c * 128 + col.shape[1]] = jnp.where(
                col == spot, 1.0, 0.0).astype(BF16)
    qc = min(256, nq)
    for c in range(nq // qc):
        cols = slice(c * qc, (c + 1) * qc)
        slots = jnp.dot(left, pm[:, cols], preferred_element_type=F32)
        block = slots[128:129]
        south = jnp.where(block >= 80.0, 1.0, 0.0)
        a = block - 80.0 * south
        side = jnp.where(a >= 40.0, 1.0, 0.0)
        ws[:128, cols] = jnp.where(side == 0.0, slots[:128], 0.0).astype(BF16)
        ws[128:, cols] = jnp.where(side == 1.0, slots[:128], 0.0).astype(BF16)
        key[:, cols] = jnp.broadcast_to((a - 40.0 * side) * 2.0 + south, (8, qc))

    a_of = (iota((40, 128), 0) >> 1).astype(F32)
    lane_of = iota((1, 128), 1).astype(F32)
    m_of, b_of = iota((128, LB), 0).astype(F32), iota((128, LB), 1).astype(F32)
    flip = 1.0 - 2.0 * (iota((128, LB), 0) & 1).astype(F32)
    for k in range(10):
        first = 256.0 * (k % 5) + k // 5
        number = 2.0 * lane_of + first
        weight = jnp.where(number == 0.0, 1.0, 2.0)
        cos_a, sin_a = cos_sin(number * a_of, 80.0)
        ca[k], sn[k] = cos_a * weight, sin_a * weight
        cos_b, sin_b = cos_sin((2.0 * m_of + first) * b_of, float(NLON))
        ba[k * 256:k * 256 + 128, :128] = cos_b.astype(BF16)
        ba[k * 256 + 128:k * 256 + 256, :128] = (-sin_b).astype(BF16)
        if k < 5:
            ba[k * 256:k * 256 + 128, 128:] = (cos_b * flip).astype(BF16)
            ba[k * 256 + 128:k * 256 + 256, 128:] = (-sin_b * flip).astype(BF16)
        else:
            ba[k * 256:k * 256 + 128, 128:] = (-sin_b * flip).astype(BF16)
            ba[k * 256 + 128:k * 256 + 256, 128:] = (-cos_b * flip).astype(BF16)

    pltpu.make_async_copy(sa.at[pl.ds(0, nw - 1)], ra.at[pl.ds(0, nw - 1)], ra_sem).wait()

    got = ra[...].astype(F32)
    re, im = got[:, 0, :], got[:, 1, :]
    re_t, im_t = jnp.transpose(re), jnp.transpose(im)
    low_lane = iota((nw, 128), 1).astype(F32)
    lefts, rights = [], []
    for m in range(mloc):
        both = jnp.concatenate([re_t[m * 8:(m + 1) * 8], im_t[m * 8:(m + 1) * 8]], axis=0)
        high = re_t[80 + m:81 + m]
        lefts.append(jnp.concatenate(
            [jnp.where(high == float(hi), both, 0.0) for hi in range(10)], axis=0).astype(BF16))
        rights.append(jnp.where(re[:, 96 + m:97 + m] == low_lane, 1.0, 0.0).astype(BF16))
    columns = jnp.dot(jnp.concatenate(lefts, axis=1), jnp.concatenate(rights, axis=0),
                      preferred_element_type=F32)

    parity = (iota((8, 128), 0) & 1) == 0
    for k in range(10):
        cos_a, sin_a = ca[k].reshape(5, 8, 128), sn[k].reshape(5, 8, 128)
        g_re, g_im = columns[k * 16:k * 16 + 8], columns[k * 16 + 8:k * 16 + 16]
        for f in range(4):
            fr = jnp.where(parity, g_re[2 * f:2 * f + 1], g_re[2 * f + 1:2 * f + 2])[None]
            fi = jnp.where(parity, g_im[2 * f:2 * f + 1], g_im[2 * f + 1:2 * f + 2])[None]
            t_re = (fr * cos_a - fi * sin_a).reshape(40, 128)
            t_im = (fr * sin_a + fi * cos_a).reshape(40, 128)
            tu[k // 5, f * 40:(f + 1) * 40, k % 5 * 256:k % 5 * 256 + 128] = t_re.astype(BF16)
            tu[k // 5, f * 40:(f + 1) * 40, k % 5 * 256 + 128:k % 5 * 256 + 256] = t_im.astype(BF16)
    scale = 1.0 / math.sqrt(2.0 * mloc * nw)
    even = jnp.dot(tu[0], ba[:1280], preferred_element_type=F32)
    odd = jnp.dot(tu[1], ba[1280:], preferred_element_type=F32)
    plus, minus = (even + odd) * scale, (even - odd) * scale
    for f in range(4):
        rows = slice(f * 40, (f + 1) * 40)
        for side, lines in enumerate((plus, minus)):
            gr[f, side * 80:(side + 1) * 80] = jnp.concatenate(
                [lines[rows, :128], lines[rows, 128:]], axis=0).astype(BF16)

    row = iota((80, qc), 0).astype(F32)
    sides = jnp.concatenate(
        [jnp.concatenate([gr[f, :80], gr[f, 80:]], axis=1) for f in range(4)], axis=0)
    for c in range(nq // qc):
        cols = slice(c * qc, (c + 1) * qc)
        hit = row == key[0:1, cols]
        prod = jnp.dot(sides, ws[:, cols], preferred_element_type=F32)
        val = jnp.concatenate(
            [jnp.sum(jnp.where(hit, prod[f * 80:(f + 1) * 80], 0.0), axis=0, keepdims=True)
             for f in range(4)], axis=0)
        high = val.astype(BF16).astype(F32)
        val = jnp.concatenate([high, val - high], axis=0)
        for j in range(qc // nw):
            s = c * (qc // nw) + j
            vs[s * 8:(s + 1) * 8] = val[:, j * nw:(j + 1) * nw]
    sb[...] = jnp.transpose(vs[...])

    def send_b(to):
        pltpu.make_async_remote_copy(
            src_ref=sb.at[pl.ds(to, 1)], dst_ref=rb.at[pl.ds(me, 1)], send_sem=sb_sem,
            recv_sem=rb_sem, device_id=(to, y), device_id_type=MESH).start()

    each_other(me, nw, send_b)
    rb[pl.ds(me, 1)] = sb[pl.ds(me, 1)]
    out = pltpu.make_async_copy(gr, grid_hbm, grid_sem)
    out.start()

    for s in range(SLOTS):
        one[s * nw:(s + 1) * nw] = jnp.where(
            im[:, 112 + s:113 + s] == low_lane, 1.0, 0.0).astype(BF16)

    pltpu.make_async_copy(sb.at[pl.ds(0, nw - 1)], rb.at[pl.ds(0, nw - 1)], rb_sem).wait()
    val = jnp.transpose(rb[...])
    named = []
    for s in range(SLOTS):
        high = im_t[96 + s:97 + s]
        named.append(jnp.concatenate(
            [jnp.where(high == float(hi), val[s * 8:(s + 1) * 8], 0.0) for hi in range(BPW // 128)],
            axis=0).astype(BF16))
    dense = jnp.dot(jnp.concatenate(named, axis=1), one[...], preferred_element_type=F32)
    dense = [dense[hi * 8:hi * 8 + 4] + dense[hi * 8 + 4:hi * 8 + 8] for hi in range(BPW // 128)]
    each = BPW // 128 // ng
    for g in range(ng):
        for k in range(each):
            sd[g, :, k * 128:(k + 1) * 128] = dense[g * each + k]
    moves = []
    for k in range(1, ng):
        to = lax.rem(y + k, ng)
        moves.append(pltpu.make_async_remote_copy(
            src_ref=sd.at[to], dst_ref=rd.at[y], send_sem=sd_sem, recv_sem=rd_sem,
            device_id=(me, to), device_id_type=MESH))
        moves[-1].start()
    rd[y] = sd[y]
    pltpu.make_async_copy(sd.at[pl.ds(0, ng - 1)], rd.at[pl.ds(0, ng - 1)], rd_sem).wait()
    sums_ref[...] = rd[...]

    out.wait()
    pltpu.make_async_copy(sa.at[pl.ds(0, nw - 1)], ra.at[pl.ds(0, nw - 1)], sa_sem).wait()
    pltpu.make_async_copy(sb.at[pl.ds(0, nw - 1)], rb.at[pl.ds(0, nw - 1)], sb_sem).wait()
    pltpu.make_async_copy(sd.at[pl.ds(0, ng - 1)], rd.at[pl.ds(0, ng - 1)], sd_sem).wait()


def per_device(spectra, legendre, wave_numbers, block_index, block_weights, basin_index):
    nw, ng = lax.axis_size("wave"), lax.axis_size("basin")
    mloc, ncoef, lats = legendre.shape
    nnz = block_index.shape[1]
    eb = min(128, nnz)
    nq = SLOTS * nw
    width = BPW // ng
    vmem = pl.BlockSpec(memory_space=pltpu.VMEM)
    grid, sums = pl.pallas_call(
        functools.partial(kernel, nw, ng),
        out_shape=(jax.ShapeDtypeStruct((4, 160, 128), BF16),
                   jax.ShapeDtypeStruct((ng, 4, width), F32)),
        in_specs=[pl.BlockSpec(memory_space=pltpu.HBM)] * 6,
        out_specs=(pl.BlockSpec(memory_space=pl.ANY), vmem),
        scratch_shapes=[
            pltpu.VMEM((4, mloc, 2, ncoef), BF16),
            pltpu.SMEM((mloc,), jnp.int32),
            pltpu.VMEM((nnz // eb, eb), jnp.int32),
            pltpu.VMEM((nnz, BLOCK), BF16),
            pltpu.VMEM((nnz // eb, eb), jnp.int32),
            pltpu.VMEM((mloc, ncoef, lats), BF16),
            pltpu.VMEM((nw, 2, 128), BF16),
            pltpu.VMEM((nw, 2, 128), BF16),
            pltpu.VMEM((nw, 128), F32),
            pltpu.VMEM((nw, 128), F32),
            pltpu.VMEM((ng, 4, width), F32),
            pltpu.VMEM((ng, 4, width), F32),
            pltpu.VMEM((2, 160, 1280), BF16),
            pltpu.VMEM((2560, 256), BF16),
            pltpu.VMEM((10, 40, 128), F32),
            pltpu.VMEM((10, 40, 128), F32),
            pltpu.VMEM((256, nq), BF16),
            pltpu.VMEM((8, nq), F32),
            pltpu.VMEM((nq, 128), BF16),
            pltpu.VMEM((128, nw), F32),
            pltpu.VMEM((4, 160, 128), BF16),
            pltpu.VMEM((nnz, nq), BF16),
            pltpu.SemaphoreType.DMA((5,)),
            pltpu.SemaphoreType.DMA((mloc,)),
            pltpu.SemaphoreType.DMA,
            pltpu.SemaphoreType.DMA,
            pltpu.SemaphoreType.DMA,
            pltpu.SemaphoreType.DMA,
            pltpu.SemaphoreType.DMA,
            pltpu.SemaphoreType.DMA,
            pltpu.SemaphoreType.DMA,
        ],
        compiler_params=pltpu.CompilerParams(
            collective_id=0, has_side_effects=True, vmem_limit_bytes=40 * 1024 * 1024),
    )(*[pltpu.with_memory_space_constraint(x, pltpu.HBM) for x in (
        jnp.transpose(spectra, (0, 2, 1, 3)), legendre, wave_numbers,
        block_index.reshape(nnz // eb, eb), block_weights.reshape(nnz, BLOCK),
        basin_index.reshape(nnz // eb, eb))])
    grid = jnp.transpose(grid.reshape(4, 80, 2, 128), (0, 2, 1, 3)).reshape(4, 2, 1, NLON)
    return grid, sums.reshape(ng * 4, width)


def solution(mesh):
    in_specs = (
        P("basin", None, "wave", None),
        P("wave", None, None),
        P("wave"),
        P("wave", None),
        P("wave", None, None),
        P("wave", None),
    )
    out_specs = (P("basin", None, "wave", None), P(None, ("wave", "basin")))
    return jax.shard_map(
        per_device, mesh=mesh, in_specs=in_specs, out_specs=out_specs, check_vma=False
    )
```

```python
import functools
import math

import jax
import jax.numpy as jnp
from jax import lax
from jax.experimental import pallas as pl
from jax.experimental.pallas import tpu as pltpu
from jax.sharding import PartitionSpec as P

NLON = 10240
LB = 128
BLOCK = 128
SLOTS = 16
BPW_BITS = 9
BPW = 1 << BPW_BITS
MESH = pl.DeviceIdType.MESH
F32 = jnp.float32
BF16 = jnp.bfloat16

COS_C = [(-1) ** n * math.pi ** (2 * n) / math.factorial(2 * n) for n in range(7)]
SIN_C = [(-1) ** n * math.pi ** (2 * n + 1) / math.factorial(2 * n + 1) for n in range(6)]


def cos_sin(r, turn):
    r = r - turn * jnp.floor(r * (1.0 / turn) + 0.5)
    y = r * (1.0 / turn)
    yy = y * y
    c = jnp.full_like(yy, COS_C[6])
    for k in range(5, -1, -1):
        c = c * yy + COS_C[k]
    s = jnp.full_like(yy, SIN_C[5])
    for k in range(4, -1, -1):
        s = s * yy + SIN_C[k]
    s = s * y
    return 1.0 - 2.0 * (s * s), 2.0 * (s * c)


def each_other(me, nw, act):
    if nw != 128:
        lax.fori_loop(1, nw, lambda k, carry: (act(lax.rem(me + k, nw)), carry)[1], 0)
        return
    x, z, c = me >> 5, (me >> 1) & 15, me & 1
    planes = [(((x + xd) & 3) << 5) | (c ^ cd) for xd in (2, 1, 3, 0) for cd in (1, 0)]

    def level(i, carry):
        there = ((z + 8 + ((i + 1) >> 1) * (2 * (i & 1) - 1)) & 15) << 1
        for plane in planes:
            act(plane | there)
        return carry

    lax.fori_loop(0, 15, level, 0)
    for plane in planes[:-1]:
        act(plane | (z << 1))


def iota(shape, dim):
    return lax.broadcasted_iota(jnp.int32, shape, dim)


def kernel(nw, ng, spec_hbm, leg_hbm, wn_hbm, blk_hbm, wgt_hbm, bas_hbm,
           grid_hbm, sums_ref,
           spec_ref, wn_ref, blk_ref, wgt_ref, bas_ref, leg, sa, ra, sb, rb, sd, rd, tu, ba, ca, sn, ws, key, one, vs, gr, spread, sm,
           in_sem, leg_sem, grid_sem, sa_sem, ra_sem, sb_sem, rb_sem, sd_sem, rd_sem):
    me, y = lax.axis_index("wave"), lax.axis_index("basin")
    mloc = leg.shape[0]
    nb, eb = bas_ref.shape
    nq = SLOTS * nw

    barrier = pltpu.get_barrier_semaphore()

    def greet(to):
        pl.semaphore_signal(barrier, inc=1, device_id=(to, y), device_id_type=MESH)

    each_other(me, nw, greet)
    for k in range(1, ng):
        pl.semaphore_signal(barrier, inc=1, device_id=(me, lax.rem(y + k, ng)), device_id_type=MESH)

    bring = [pltpu.make_async_copy(*pair, in_sem.at[i]) for i, pair in enumerate((
        (bas_hbm, bas_ref), (spec_hbm, spec_ref), (wn_hbm, wn_ref), (blk_hbm, blk_ref),
        (wgt_hbm, wgt_ref)))]
    for copy in bring[:2]:
        copy.start()
    for m in range(mloc):
        pltpu.make_async_copy(leg_hbm.at[m], leg.at[m], leg_sem.at[m]).start()
    for copy in bring[2:]:
        copy.start()

    bring[0].wait()
    bas = bas_ref[...]
    owner = bas >> BPW_BITS
    local = bas & (BPW - 1)
    upper = (iota((eb, eb), 0) < iota((eb, eb), 1)).astype(F32).astype(BF16)
    owned = [(owner[i:i + 1] == iota((nw, eb), 0)).astype(F32) for i in range(nb)]
    before = jnp.zeros((nw, 1), F32)
    ranks = []
    for i in range(nb):
        inside = jnp.dot(owned[i].astype(BF16), upper, preferred_element_type=F32)
        ranks.append(jnp.sum(owned[i] * (inside + before), axis=0, keepdims=True))
        before = before + jnp.sum(owned[i], axis=1, keepdims=True)
    lane = iota((128, eb), 0)
    where_to = jnp.zeros((nw, 128), F32)
    for i in range(nb):
        high = (local[i:i + 1] >> 7).astype(F32)
        low = (local[i:i + 1] & 127).astype(F32)
        rank = ranks[i].astype(jnp.int32)
        named = jnp.where(lane == rank + 96, high, 0.0) + jnp.where(lane == rank + 112, low, 0.0)
        where_to = where_to + lax.dot_general(
            owned[i].astype(BF16), named.astype(BF16), (((1,), (1,)), ((), ())),
            preferred_element_type=F32)
    rank_rows = jnp.concatenate(ranks, axis=0)
    place = rank_rows * float(nw) + owner.astype(F32)
    place_cols = jnp.transpose(place)

    ncoef = spec_ref.shape[3]
    odd = lax.rem(iota((8, ncoef), 1), 2) == 1
    bring[1].wait()

    def column(m, carry):
        rows = jnp.concatenate([spec_ref[f, m].astype(F32) for f in range(4)], axis=0)
        both = jnp.concatenate([rows, jnp.where(odd, -rows, rows)], axis=0).astype(BF16)
        pltpu.make_async_copy(leg_hbm.at[m], leg.at[m], leg_sem.at[m]).wait()
        sm[pl.ds(pl.multiple_of(m * 16, 16), 16)] = jnp.dot(
            both, leg[m], preferred_element_type=F32)
        return carry

    lax.fori_loop(0, mloc, column, 0)
    sums = sm[...]
    if mloc * 16 % 128:
        sums = jnp.concatenate([sums, jnp.zeros((256 - mloc * 16, nw), F32)], axis=0)
    by_lat = jnp.transpose(sums).astype(BF16)
    src = iota((256, 256), 0)
    dst = iota((256, 256), 1)
    r_of, lane_of = dst >> 7, dst & 127
    m_of, f_of, h_of = lane_of >> 3, (lane_of >> 1) & 3, lane_of & 1
    pick = (src == m_of * 16 + h_of * 8 + f_of * 2 + r_of) & (lane_of < mloc * 8)
    ordered = jnp.dot(by_lat, pick.astype(F32).astype(BF16), preferred_element_type=F32)
    lane = iota((1, 128), 1)
    numbers = jnp.zeros((1, 128), F32)
    bring[2].wait()
    for m in range(mloc):
        wn = wn_ref[m]
        chunk = (wn & 1) * 5 + (wn >> 8)
        numbers = numbers + jnp.where(lane == 80 + m, chunk.astype(F32), 0.0)
        numbers = numbers + jnp.where(lane == 96 + m, ((wn >> 1) & 127).astype(F32), 0.0)
    part_re = ordered[:, :128] + numbers
    part_im = ordered[:, 128:] + where_to
    sa[...] = jnp.concatenate([part_re[:, None, :], part_im[:, None, :]], axis=1).astype(BF16)

    pl.semaphore_wait(barrier, nw - 1 + ng - 1)

    def send_a(to):
        pltpu.make_async_remote_copy(
            src_ref=sa.at[pl.ds(to, 1)], dst_ref=ra.at[pl.ds(me, 1)], send_sem=sa_sem,
            recv_sem=ra_sem, device_id=(to, y), device_id_type=MESH).start()

    each_other(me, nw, send_a)
    ra[pl.ds(me, 1)] = sa[pl.ds(me, 1)]

    bring[3].wait()
    bring[4].wait()
    ext = jnp.concatenate(
        [jnp.concatenate([blk_ref[i:i + 1].astype(F32), jnp.zeros((15, eb), F32)], axis=0)
         for i in range(nb)], axis=1)
    turned_w = jnp.concatenate(
        [jnp.transpose(wgt_ref[i * eb:(i + 1) * eb].astype(F32)) for i in range(nb)], axis=1)
    left = jnp.concatenate([turned_w, ext], axis=0).astype(BF16)
    qc = min(256, nq)
    for i in range(nb):
        spread[i * eb:(i + 1) * eb] = jnp.broadcast_to(place_cols[:, i:i + 1], (eb, qc))
    spot = iota((1, qc), 1).astype(F32)

    def put(c, carry):
        cols = pl.ds(pl.multiple_of(c * qc, qc), qc)
        placed = jnp.where(spread[...] == spot + (c * qc).astype(F32), 1.0, 0.0).astype(BF16)
        slots = jnp.dot(left, placed, preferred_element_type=F32)
        block = slots[128:129]
        south = jnp.where(block >= 80.0, 1.0, 0.0)
        a = block - 80.0 * south
        side = jnp.where(a >= 40.0, 1.0, 0.0)
        ws[:128, cols] = jnp.where(side == 0.0, slots[:128], 0.0).astype(BF16)
        ws[128:, cols] = jnp.where(side == 1.0, slots[:128], 0.0).astype(BF16)
        key[:, cols] = jnp.broadcast_to((a - 40.0 * side) * 2.0 + south, (8, qc))
        return carry

    lax.fori_loop(0, nq // qc, put, 0)

    a_of = (iota((40, 128), 0) >> 1).astype(F32)
    lane_of = iota((1, 128), 1).astype(F32)
    m_of, b_of = iota((128, LB), 0).astype(F32), iota((128, LB), 1).astype(F32)
    flip = 1.0 - 2.0 * (iota((128, LB), 0) & 1).astype(F32)

    def table(k, carry):
        is_odd = k >= 5
        odd_one = is_odd.astype(jnp.int32)
        first = ((k - 5 * odd_one) * 256 + odd_one).astype(F32)
        number = 2.0 * lane_of + first
        weight = jnp.where(number == 0.0, 1.0, 2.0)
        cos_a, sin_a = cos_sin(number * a_of, 80.0)
        ca[k], sn[k] = cos_a * weight, sin_a * weight
        cos_b, sin_b = cos_sin((2.0 * m_of + first) * b_of, float(NLON))
        row = pl.multiple_of(k * 256, 256)
        ba[pl.ds(row, 128), :128] = cos_b.astype(BF16)
        ba[pl.ds(row + 128, 128), :128] = (-sin_b).astype(BF16)
        ba[pl.ds(row, 128), 128:] = (jnp.where(is_odd, -sin_b, cos_b) * flip).astype(BF16)
        ba[pl.ds(row + 128, 128), 128:] = (jnp.where(is_odd, -cos_b, -sin_b) * flip).astype(BF16)
        return carry

    lax.fori_loop(0, 10, table, 0)

    pltpu.make_async_copy(sa.at[pl.ds(0, nw - 1)], ra.at[pl.ds(0, nw - 1)], ra_sem).wait()

    got = ra[...].astype(F32)
    re, im = got[:, 0, :], got[:, 1, :]
    re_t, im_t = jnp.transpose(re), jnp.transpose(im)
    low_row = iota((128, nw), 0).astype(F32)
    lefts, rights = [], []
    for m in range(mloc):
        both = jnp.concatenate([re_t[m * 8:(m + 1) * 8], im_t[m * 8:(m + 1) * 8]], axis=0)
        high = re_t[80 + m:81 + m]
        lefts.append(jnp.concatenate(
            [jnp.where(high == float(hi), both, 0.0) for hi in range(10)], axis=0).astype(BF16))
        rights.append(jnp.where(re_t[96 + m:97 + m] == low_row, 1.0, 0.0).astype(BF16))
    columns = lax.dot_general(
        jnp.concatenate(lefts, axis=1), jnp.concatenate(rights, axis=1), (((1,), (1,)), ((), ())),
        preferred_element_type=F32)

    parity = (iota((8, 128), 0) & 1) == 0
    for k in range(10):
        cos_a, sin_a = ca[k].reshape(5, 8, 128), sn[k].reshape(5, 8, 128)
        g_re, g_im = columns[k * 16:k * 16 + 8], columns[k * 16 + 8:k * 16 + 16]
        for f in range(4):
            fr = jnp.where(parity, g_re[2 * f:2 * f + 1], g_re[2 * f + 1:2 * f + 2])[None]
            fi = jnp.where(parity, g_im[2 * f:2 * f + 1], g_im[2 * f + 1:2 * f + 2])[None]
            t_re = (fr * cos_a - fi * sin_a).reshape(40, 128)
            t_im = (fr * sin_a + fi * cos_a).reshape(40, 128)
            tu[k // 5, f * 40:(f + 1) * 40, k % 5 * 256:k % 5 * 256 + 128] = t_re.astype(BF16)
            tu[k // 5, f * 40:(f + 1) * 40, k % 5 * 256 + 128:k % 5 * 256 + 256] = t_im.astype(BF16)
    scale = 1.0 / math.sqrt(2.0 * mloc * nw)
    even = jnp.dot(tu[0], ba[:1280], preferred_element_type=F32)
    odd = jnp.dot(tu[1], ba[1280:], preferred_element_type=F32)
    plus, minus = (even + odd) * scale, (even - odd) * scale
    for f in range(4):
        rows = slice(f * 40, (f + 1) * 40)
        for side, lines in enumerate((plus, minus)):
            gr[f, side * 80:(side + 1) * 80] = jnp.concatenate(
                [lines[rows, :128], lines[rows, 128:]], axis=0).astype(BF16)

    row = iota((80, qc), 0).astype(F32)
    sides = jnp.concatenate(
        [jnp.concatenate([gr[f, :80], gr[f, 80:]], axis=1) for f in range(4)], axis=0)
    for c in range(nq // qc):
        cols = slice(c * qc, (c + 1) * qc)
        hit = row == key[0:1, cols]
        prod = jnp.dot(sides, ws[:, cols], preferred_element_type=F32)
        val = jnp.concatenate(
            [jnp.sum(jnp.where(hit, prod[f * 80:(f + 1) * 80], 0.0), axis=0, keepdims=True)
             for f in range(4)], axis=0)
        high = val.astype(BF16).astype(F32)
        val = jnp.concatenate([high, val - high], axis=0)
        for j in range(qc // nw):
            s = c * (qc // nw) + j
            vs[s * 8:(s + 1) * 8] = val[:, j * nw:(j + 1) * nw]
    sb[...] = jnp.transpose(vs[...])

    def send_b(to):
        pltpu.make_async_remote_copy(
            src_ref=sb.at[pl.ds(to, 1)], dst_ref=rb.at[pl.ds(me, 1)], send_sem=sb_sem,
            recv_sem=rb_sem, device_id=(to, y), device_id_type=MESH).start()

    each_other(me, nw, send_b)
    rb[pl.ds(me, 1)] = sb[pl.ds(me, 1)]
    out = pltpu.make_async_copy(gr, grid_hbm, grid_sem)
    out.start()

    for s in range(SLOTS):
        one[:, s * nw:(s + 1) * nw] = jnp.where(
            im_t[112 + s:113 + s] == low_row, 1.0, 0.0).astype(BF16)

    pltpu.make_async_copy(sb.at[pl.ds(0, nw - 1)], rb.at[pl.ds(0, nw - 1)], rb_sem).wait()
    val = jnp.transpose(rb[...])
    named = []
    for s in range(SLOTS):
        high = im_t[96 + s:97 + s]
        named.append(jnp.concatenate(
            [jnp.where(high == float(hi), val[s * 8:(s + 1) * 8], 0.0) for hi in range(BPW // 128)],
            axis=0).astype(BF16))
    dense = lax.dot_general(jnp.concatenate(named, axis=1), one[...], (((1,), (1,)), ((), ())),
                            preferred_element_type=F32)
    dense = [dense[hi * 8:hi * 8 + 4] + dense[hi * 8 + 4:hi * 8 + 8] for hi in range(BPW // 128)]
    each = BPW // 128 // ng
    for g in range(ng):
        for k in range(each):
            sd[g, :, k * 128:(k + 1) * 128] = dense[g * each + k]
    moves = []
    for k in sorted(range(1, ng), key=lambda k: abs(2 * k - ng)):
        to = lax.rem(y + k, ng)
        moves.append(pltpu.make_async_remote_copy(
            src_ref=sd.at[to], dst_ref=rd.at[y], send_sem=sd_sem, recv_sem=rd_sem,
            device_id=(me, to), device_id_type=MESH))
        moves[-1].start()
    rd[y] = sd[y]
    pltpu.make_async_copy(sd.at[pl.ds(0, ng - 1)], rd.at[pl.ds(0, ng - 1)], rd_sem).wait()
    sums_ref[...] = rd[...]

    out.wait()
    pltpu.make_async_copy(sa.at[pl.ds(0, nw - 1)], ra.at[pl.ds(0, nw - 1)], sa_sem).wait()
    pltpu.make_async_copy(sb.at[pl.ds(0, nw - 1)], rb.at[pl.ds(0, nw - 1)], sb_sem).wait()
    pltpu.make_async_copy(sd.at[pl.ds(0, ng - 1)], rd.at[pl.ds(0, ng - 1)], sd_sem).wait()


def per_device(spectra, legendre, wave_numbers, block_index, block_weights, basin_index):
    nw, ng = lax.axis_size("wave"), lax.axis_size("basin")
    mloc, ncoef, lats = legendre.shape
    nnz = block_index.shape[1]
    eb = min(128, nnz)
    nq = SLOTS * nw
    width = BPW // ng
    vmem = pl.BlockSpec(memory_space=pltpu.VMEM)
    grid, sums = pl.pallas_call(
        functools.partial(kernel, nw, ng),
        out_shape=(jax.ShapeDtypeStruct((4, 160, 128), BF16),
                   jax.ShapeDtypeStruct((ng, 4, width), F32)),
        in_specs=[pl.BlockSpec(memory_space=pltpu.HBM)] * 6,
        out_specs=(pl.BlockSpec(memory_space=pl.ANY), vmem),
        scratch_shapes=[
            pltpu.VMEM((4, mloc, 2, ncoef), BF16),
            pltpu.SMEM((mloc,), jnp.int32),
            pltpu.VMEM((nnz // eb, eb), jnp.int32),
            pltpu.VMEM((nnz, BLOCK), BF16),
            pltpu.VMEM((nnz // eb, eb), jnp.int32),
            pltpu.VMEM((mloc, ncoef, lats), BF16),
            pltpu.VMEM((nw, 2, 128), BF16),
            pltpu.VMEM((nw, 2, 128), BF16),
            pltpu.VMEM((nw, 128), F32),
            pltpu.VMEM((nw, 128), F32),
            pltpu.VMEM((ng, 4, width), F32),
            pltpu.VMEM((ng, 4, width), F32),
            pltpu.VMEM((2, 160, 1280), BF16),
            pltpu.VMEM((2560, 256), BF16),
            pltpu.VMEM((10, 40, 128), F32),
            pltpu.VMEM((10, 40, 128), F32),
            pltpu.VMEM((256, nq), BF16),
            pltpu.VMEM((8, nq), F32),
            pltpu.VMEM((128, nq), BF16),
            pltpu.VMEM((128, nw), F32),
            pltpu.VMEM((4, 160, 128), BF16),
            pltpu.VMEM((nnz, min(256, nq)), F32),
            pltpu.VMEM((16 * mloc, nw), F32),
            pltpu.SemaphoreType.DMA((5,)),
            pltpu.SemaphoreType.DMA((mloc,)),
            pltpu.SemaphoreType.DMA,
            pltpu.SemaphoreType.DMA,
            pltpu.SemaphoreType.DMA,
            pltpu.SemaphoreType.DMA,
            pltpu.SemaphoreType.DMA,
            pltpu.SemaphoreType.DMA,
            pltpu.SemaphoreType.DMA,
        ],
        compiler_params=pltpu.CompilerParams(
            collective_id=0, has_side_effects=True, vmem_limit_bytes=40 * 1024 * 1024),
    )(*[pltpu.with_memory_space_constraint(x, pltpu.HBM) for x in (
        jnp.transpose(spectra, (0, 2, 1, 3)), legendre, wave_numbers,
        block_index.reshape(nnz // eb, eb), block_weights.reshape(nnz, BLOCK),
        basin_index.reshape(nnz // eb, eb))])
    grid = jnp.transpose(grid.reshape(4, 80, 2, 128), (0, 2, 1, 3)).reshape(4, 2, 1, NLON)
    return grid, sums.reshape(ng * 4, width)


def solution(mesh):
    in_specs = (
        P("basin", None, "wave", None),
        P("wave", None, None),
        P("wave"),
        P("wave", None),
        P("wave", None, None),
        P("wave", None),
    )
    out_specs = (P("basin", None, "wave", None), P(None, ("wave", "basin")))
    return jax.shard_map(
        per_device, mesh=mesh, in_specs=in_specs, out_specs=out_specs, check_vma=False
    )
```

```python
import functools
import math

import jax
import jax.numpy as jnp
from jax import lax
from jax.experimental import pallas as pl
from jax.experimental.pallas import tpu as pltpu
from jax.sharding import PartitionSpec as P

NLON = 10240
LB = 128
BLOCK = 128
SLOTS = 16
BPW_BITS = 9
BPW = 1 << BPW_BITS
MESH = pl.DeviceIdType.MESH
F32 = jnp.float32
BF16 = jnp.bfloat16

COS_C = [(-1) ** n * math.pi ** (2 * n) / math.factorial(2 * n) for n in range(7)]
SIN_C = [(-1) ** n * math.pi ** (2 * n + 1) / math.factorial(2 * n + 1) for n in range(6)]


def cos_sin(r, turn):
    r = r - turn * jnp.floor(r * (1.0 / turn) + 0.5)
    y = r * (1.0 / turn)
    yy = y * y
    c = jnp.full_like(yy, COS_C[6])
    for k in range(5, -1, -1):
        c = c * yy + COS_C[k]
    s = jnp.full_like(yy, SIN_C[5])
    for k in range(4, -1, -1):
        s = s * yy + SIN_C[k]
    s = s * y
    return 1.0 - 2.0 * (s * s), 2.0 * (s * c)


def each_other(me, nw, act):
    if nw != 128:
        lax.fori_loop(1, nw, lambda k, carry: (act(lax.rem(me + k, nw)), carry)[1], 0)
        return
    x, z, c = me >> 5, (me >> 1) & 15, me & 1
    planes = [(((x + xd) & 3) << 5) | (c ^ cd) for xd in (2, 1, 3, 0) for cd in (1, 0)]

    def level(i, carry):
        there = ((z + 8 + ((i + 1) >> 1) * (2 * (i & 1) - 1)) & 15) << 1
        for plane in planes:
            act(plane | there)
        return carry

    lax.fori_loop(0, 15, level, 0, unroll=5)
    for plane in planes[:-1]:
        act(plane | (z << 1))


def iota(shape, dim):
    return lax.broadcasted_iota(jnp.int32, shape, dim)


def kernel(nw, ng, spec_hbm, leg_hbm, wn_hbm, blk_hbm, wgt_hbm, bas_hbm,
           grid_hbm, sums_hbm,
           spec_ref, wn_ref, blk_ref, wgt_ref, bas_ref, leg, sa, ra, sb, rb, sd, tu, ba, ca, sn, ws, key, one, vs, gr, spread, sm,
           in_sem, leg_sem, grid_sem, sa_sem, ra_sem, sb_sem, rb_sem, sd_sem, rd_sem, own_sem):
    me, y = lax.axis_index("wave"), lax.axis_index("basin")
    mloc = leg.shape[0]
    nb, eb = bas_ref.shape
    nq = SLOTS * nw

    barrier = pltpu.get_barrier_semaphore()

    def greet(to):
        pl.semaphore_signal(barrier, inc=1, device_id=(to, y), device_id_type=MESH)

    each_other(me, nw, greet)
    for k in range(1, ng):
        pl.semaphore_signal(barrier, inc=1, device_id=(me, lax.rem(y + k, ng)), device_id_type=MESH)

    bring = [pltpu.make_async_copy(*pair, in_sem.at[i]) for i, pair in enumerate((
        (bas_hbm, bas_ref), (spec_hbm, spec_ref), (wn_hbm, wn_ref), (blk_hbm, blk_ref),
        (wgt_hbm, wgt_ref)))]
    for copy in bring[:2]:
        copy.start()
    for m in range(mloc):
        pltpu.make_async_copy(leg_hbm.at[m], leg.at[m], leg_sem.at[m]).start()
    for copy in bring[2:]:
        copy.start()

    bring[0].wait()
    bas = bas_ref[...]
    owner = bas >> BPW_BITS
    local = bas & (BPW - 1)
    upper = (iota((eb, eb), 0) < iota((eb, eb), 1)).astype(F32).astype(BF16)
    owned = [(owner[i:i + 1] == iota((nw, eb), 0)).astype(F32) for i in range(nb)]
    before = jnp.zeros((nw, 1), F32)
    ranks = []
    for i in range(nb):
        inside = jnp.dot(owned[i].astype(BF16), upper, preferred_element_type=F32)
        ranks.append(jnp.sum(owned[i] * (inside + before), axis=0, keepdims=True))
        before = before + jnp.sum(owned[i], axis=1, keepdims=True)
    lane = iota((128, eb), 0)
    where_to = jnp.zeros((nw, 128), F32)
    for i in range(nb):
        high = (local[i:i + 1] >> 7).astype(F32)
        low = (local[i:i + 1] & 127).astype(F32)
        rank = ranks[i].astype(jnp.int32)
        named = jnp.where(lane == rank + 96, high, 0.0) + jnp.where(lane == rank + 112, low, 0.0)
        where_to = where_to + lax.dot_general(
            owned[i].astype(BF16), named.astype(BF16), (((1,), (1,)), ((), ())),
            preferred_element_type=F32)
    rank_rows = jnp.concatenate(ranks, axis=0)
    place = rank_rows * float(nw) + owner.astype(F32)
    place_cols = jnp.transpose(place)

    ncoef = spec_ref.shape[3]
    odd = lax.rem(iota((8, ncoef), 1), 2) == 1
    bring[1].wait()

    def column(m, carry):
        rows = jnp.concatenate([spec_ref[f, m].astype(F32) for f in range(4)], axis=0)
        both = jnp.concatenate([rows, jnp.where(odd, -rows, rows)], axis=0).astype(BF16)
        pltpu.make_async_copy(leg_hbm.at[m], leg.at[m], leg_sem.at[m]).wait()
        sm[pl.ds(pl.multiple_of(m * 16, 16), 16)] = jnp.dot(
            both, leg[m], preferred_element_type=F32)
        return carry

    lax.fori_loop(0, mloc, column, 0)
    sums = sm[...]
    if mloc * 16 % 128:
        sums = jnp.concatenate([sums, jnp.zeros((256 - mloc * 16, nw), F32)], axis=0)
    by_lat = jnp.transpose(sums).astype(BF16)
    src = iota((256, 256), 0)
    dst = iota((256, 256), 1)
    r_of, lane_of = dst >> 7, dst & 127
    m_of, f_of, h_of = lane_of >> 3, (lane_of >> 1) & 3, lane_of & 1
    pick = (src == m_of * 16 + h_of * 8 + f_of * 2 + r_of) & (lane_of < mloc * 8)
    ordered = jnp.dot(by_lat, pick.astype(F32).astype(BF16), preferred_element_type=F32)
    lane = iota((1, 128), 1)
    numbers = jnp.zeros((1, 128), F32)
    bring[2].wait()
    for m in range(mloc):
        wn = wn_ref[m]
        chunk = (wn & 1) * 5 + (wn >> 8)
        numbers = numbers + jnp.where(lane == 80 + m, chunk.astype(F32), 0.0)
        numbers = numbers + jnp.where(lane == 96 + m, ((wn >> 1) & 127).astype(F32), 0.0)
    part_re = ordered[:, :128] + numbers
    part_im = ordered[:, 128:] + where_to
    sa[...] = jnp.concatenate([part_re[:, None, :], part_im[:, None, :]], axis=1).astype(BF16)

    pl.semaphore_wait(barrier, nw - 1 + ng - 1)

    def send_a(to):
        pltpu.make_async_remote_copy(
            src_ref=sa.at[pl.ds(to, 1)], dst_ref=ra.at[pl.ds(me, 1)], send_sem=sa_sem,
            recv_sem=ra_sem, device_id=(to, y), device_id_type=MESH).start()

    each_other(me, nw, send_a)
    ra[pl.ds(me, 1)] = sa[pl.ds(me, 1)]

    bring[3].wait()
    bring[4].wait()
    ext = jnp.concatenate(
        [jnp.concatenate([blk_ref[i:i + 1].astype(F32), jnp.zeros((15, eb), F32)], axis=0)
         for i in range(nb)], axis=1)
    turned_w = jnp.concatenate(
        [jnp.transpose(wgt_ref[i * eb:(i + 1) * eb].astype(F32)) for i in range(nb)], axis=1)
    left = jnp.concatenate([turned_w, ext], axis=0).astype(BF16)
    qc = min(256, nq)
    for i in range(nb):
        spread[i * eb:(i + 1) * eb] = jnp.broadcast_to(place_cols[:, i:i + 1], (eb, qc))
    spot = iota((1, qc), 1).astype(F32)

    def put(c, carry):
        cols = pl.ds(pl.multiple_of(c * qc, qc), qc)
        placed = jnp.where(spread[...] == spot + (c * qc).astype(F32), 1.0, 0.0).astype(BF16)
        slots = jnp.dot(left, placed, preferred_element_type=F32)
        block = slots[128:129]
        south = jnp.where(block >= 80.0, 1.0, 0.0)
        a = block - 80.0 * south
        side = jnp.where(a >= 40.0, 1.0, 0.0)
        ws[:128, cols] = jnp.where(side == 0.0, slots[:128], 0.0).astype(BF16)
        ws[128:, cols] = jnp.where(side == 1.0, slots[:128], 0.0).astype(BF16)
        key[:, cols] = jnp.broadcast_to((a - 40.0 * side) * 2.0 + south, (8, qc))
        return carry

    lax.fori_loop(0, nq // qc, put, 0)

    a_of = (iota((40, 128), 0) >> 1).astype(F32)
    lane_of = iota((1, 128), 1).astype(F32)
    m_of, b_of = iota((128, LB), 0).astype(F32), iota((128, LB), 1).astype(F32)
    flip = 1.0 - 2.0 * (iota((128, LB), 0) & 1).astype(F32)

    def table(k, carry):
        is_odd = k >= 5
        odd_one = is_odd.astype(jnp.int32)
        first = ((k - 5 * odd_one) * 256 + odd_one).astype(F32)
        number = 2.0 * lane_of + first
        weight = jnp.where(number == 0.0, 1.0, 2.0)
        cos_a, sin_a = cos_sin(number * a_of, 80.0)
        ca[k], sn[k] = cos_a * weight, sin_a * weight
        cos_b, sin_b = cos_sin((2.0 * m_of + first) * b_of, float(NLON))
        row = pl.multiple_of(k * 256, 256)
        ba[pl.ds(row, 128), :128] = cos_b.astype(BF16)
        ba[pl.ds(row + 128, 128), :128] = (-sin_b).astype(BF16)
        ba[pl.ds(row, 128), 128:] = (jnp.where(is_odd, -sin_b, cos_b) * flip).astype(BF16)
        ba[pl.ds(row + 128, 128), 128:] = (jnp.where(is_odd, -cos_b, -sin_b) * flip).astype(BF16)
        return carry

    lax.fori_loop(0, 10, table, 0)

    pltpu.make_async_copy(sa.at[pl.ds(0, nw - 1)], ra.at[pl.ds(0, nw - 1)], ra_sem).wait()

    re, im = ra[:, 0, :].astype(F32), ra[:, 1, :].astype(F32)
    re_t, im_t = jnp.transpose(re), jnp.transpose(im)
    low_row = iota((128, nw), 0).astype(F32)
    lefts, rights = [], []
    for m in range(mloc):
        both = jnp.concatenate([re_t[m * 8:(m + 1) * 8], im_t[m * 8:(m + 1) * 8]], axis=0)
        high = re_t[80 + m:81 + m]
        lefts.append(jnp.concatenate(
            [jnp.where(high == float(hi), both, 0.0) for hi in range(10)], axis=0).astype(BF16))
        rights.append(jnp.where(re_t[96 + m:97 + m] == low_row, 1.0, 0.0).astype(BF16))
    columns = lax.dot_general(
        jnp.concatenate(lefts, axis=1), jnp.concatenate(rights, axis=1), (((1,), (1,)), ((), ())),
        preferred_element_type=F32)

    parity = (iota((8, 128), 0) & 1) == 0
    for k in range(10):
        cos_a, sin_a = ca[k].reshape(5, 8, 128), sn[k].reshape(5, 8, 128)
        g_re, g_im = columns[k * 16:k * 16 + 8], columns[k * 16 + 8:k * 16 + 16]
        for f in range(4):
            fr = jnp.where(parity, g_re[2 * f:2 * f + 1], g_re[2 * f + 1:2 * f + 2])[None]
            fi = jnp.where(parity, g_im[2 * f:2 * f + 1], g_im[2 * f + 1:2 * f + 2])[None]
            t_re = (fr * cos_a - fi * sin_a).reshape(40, 128)
            t_im = (fr * sin_a + fi * cos_a).reshape(40, 128)
            tu[k // 5, f * 40:(f + 1) * 40, k % 5 * 256:k % 5 * 256 + 128] = t_re.astype(BF16)
            tu[k // 5, f * 40:(f + 1) * 40, k % 5 * 256 + 128:k % 5 * 256 + 256] = t_im.astype(BF16)
    scale = 1.0 / math.sqrt(2.0 * mloc * nw)
    even = jnp.dot(tu[0], ba[:1280], preferred_element_type=F32)
    odd = jnp.dot(tu[1], ba[1280:], preferred_element_type=F32)
    plus, minus = (even + odd) * scale, (even - odd) * scale
    for f in range(4):
        rows = slice(f * 40, (f + 1) * 40)
        for side, lines in enumerate((plus, minus)):
            gr[f, side * 80:(side + 1) * 80] = jnp.concatenate(
                [lines[rows, :128], lines[rows, 128:]], axis=0).astype(BF16)

    row = iota((80, qc), 0).astype(F32)
    sides = jnp.concatenate(
        [jnp.concatenate([gr[f, :80], gr[f, 80:]], axis=1) for f in range(4)], axis=0)
    for c in range(nq // qc):
        cols = slice(c * qc, (c + 1) * qc)
        hit = row == key[0:1, cols]
        prod = jnp.dot(sides, ws[:, cols], preferred_element_type=F32)
        val = jnp.concatenate(
            [jnp.sum(jnp.where(hit, prod[f * 80:(f + 1) * 80], 0.0), axis=0, keepdims=True)
             for f in range(4)], axis=0)
        high = val.astype(BF16).astype(F32)
        val = jnp.concatenate([high, val - high], axis=0)
        for j in range(qc // nw):
            s = c * (qc // nw) + j
            vs[s * 8:(s + 1) * 8] = val[:, j * nw:(j + 1) * nw]
    sb[...] = jnp.transpose(vs[...])

    def send_b(to):
        pltpu.make_async_remote_copy(
            src_ref=sb.at[pl.ds(to, 1)], dst_ref=rb.at[pl.ds(me, 1)], send_sem=sb_sem,
            recv_sem=rb_sem, device_id=(to, y), device_id_type=MESH).start()

    each_other(me, nw, send_b)
    rb[pl.ds(me, 1)] = sb[pl.ds(me, 1)]
    out = pltpu.make_async_copy(gr, grid_hbm, grid_sem)
    out.start()

    for s in range(SLOTS):
        one[:, s * nw:(s + 1) * nw] = jnp.where(
            im_t[112 + s:113 + s] == low_row, 1.0, 0.0).astype(BF16)

    pltpu.make_async_copy(sb.at[pl.ds(0, nw - 1)], rb.at[pl.ds(0, nw - 1)], rb_sem).wait()
    val = jnp.transpose(rb[...])
    named = []
    for s in range(SLOTS):
        high = im_t[96 + s:97 + s]
        named.append(jnp.concatenate(
            [jnp.where(high == float(hi), val[s * 8:(s + 1) * 8], 0.0) for hi in range(BPW // 128)],
            axis=0).astype(BF16))
    dense = lax.dot_general(jnp.concatenate(named, axis=1), one[...], (((1,), (1,)), ((), ())),
                            preferred_element_type=F32)
    dense = [dense[hi * 8:hi * 8 + 4] + dense[hi * 8 + 4:hi * 8 + 8] for hi in range(BPW // 128)]
    each = BPW // 128 // ng
    for g in range(ng):
        for k in range(each):
            sd[g, :, k * 128:(k + 1) * 128] = dense[g * each + k]
    moves = []
    for k in sorted(range(1, ng), key=lambda k: abs(2 * k - ng)):
        to = lax.rem(y + k, ng)
        moves.append(pltpu.make_async_remote_copy(
            src_ref=sd.at[to], dst_ref=sums_hbm.at[y], send_sem=sd_sem, recv_sem=rd_sem,
            device_id=(me, to), device_id_type=MESH))
        moves[-1].start()
    own = pltpu.make_async_copy(sd.at[y], sums_hbm.at[y], own_sem)
    own.start()
    pltpu.make_async_copy(sd.at[pl.ds(0, ng - 1)], sums_hbm.at[pl.ds(0, ng - 1)], rd_sem).wait()
    own.wait()

    out.wait()
    pltpu.make_async_copy(sa.at[pl.ds(0, nw - 1)], ra.at[pl.ds(0, nw - 1)], sa_sem).wait()
    pltpu.make_async_copy(sb.at[pl.ds(0, nw - 1)], rb.at[pl.ds(0, nw - 1)], sb_sem).wait()
    pltpu.make_async_copy(sd.at[pl.ds(0, ng - 1)], sums_hbm.at[pl.ds(0, ng - 1)], sd_sem).wait()


def per_device(spectra, legendre, wave_numbers, block_index, block_weights, basin_index):
    nw, ng = lax.axis_size("wave"), lax.axis_size("basin")
    mloc, ncoef, lats = legendre.shape
    nnz = block_index.shape[1]
    eb = min(128, nnz)
    nq = SLOTS * nw
    width = BPW // ng
    grid, sums = pl.pallas_call(
        functools.partial(kernel, nw, ng),
        out_shape=(jax.ShapeDtypeStruct((4, 160, 128), BF16),
                   jax.ShapeDtypeStruct((ng, 4, width), F32)),
        in_specs=[pl.BlockSpec(memory_space=pltpu.HBM)] * 6,
        out_specs=(pl.BlockSpec(memory_space=pl.ANY), pl.BlockSpec(memory_space=pl.ANY)),
        scratch_shapes=[
            pltpu.VMEM((4, mloc, 2, ncoef), BF16),
            pltpu.SMEM((mloc,), jnp.int32),
            pltpu.VMEM((nnz // eb, eb), jnp.int32),
            pltpu.VMEM((nnz, BLOCK), BF16),
            pltpu.VMEM((nnz // eb, eb), jnp.int32),
            pltpu.VMEM((mloc, ncoef, lats), BF16),
            pltpu.VMEM((nw, 2, 128), BF16),
            pltpu.VMEM((nw, 2, 128), BF16),
            pltpu.VMEM((nw, 128), F32),
            pltpu.VMEM((nw, 128), F32),
            pltpu.VMEM((ng, 4, width), F32),
            pltpu.VMEM((2, 160, 1280), BF16),
            pltpu.VMEM((2560, 256), BF16),
            pltpu.VMEM((10, 40, 128), F32),
            pltpu.VMEM((10, 40, 128), F32),
            pltpu.VMEM((256, nq), BF16),
            pltpu.VMEM((8, nq), F32),
            pltpu.VMEM((128, nq), BF16),
            pltpu.VMEM((128, nw), F32),
            pltpu.VMEM((4, 160, 128), BF16),
            pltpu.VMEM((nnz, min(256, nq)), F32),
            pltpu.VMEM((16 * mloc, nw), F32),
            pltpu.SemaphoreType.DMA((5,)),
            pltpu.SemaphoreType.DMA((mloc,)),
            pltpu.SemaphoreType.DMA,
            pltpu.SemaphoreType.DMA,
            pltpu.SemaphoreType.DMA,
            pltpu.SemaphoreType.DMA,
            pltpu.SemaphoreType.DMA,
            pltpu.SemaphoreType.DMA,
            pltpu.SemaphoreType.DMA,
            pltpu.SemaphoreType.DMA,
        ],
        compiler_params=pltpu.CompilerParams(
            collective_id=0, has_side_effects=True, vmem_limit_bytes=40 * 1024 * 1024),
    )(*[pltpu.with_memory_space_constraint(x, pltpu.HBM) for x in (
        jnp.transpose(spectra, (0, 2, 1, 3)), legendre, wave_numbers,
        block_index.reshape(nnz // eb, eb), block_weights.reshape(nnz, BLOCK),
        basin_index.reshape(nnz // eb, eb))])
    grid = jnp.transpose(grid.reshape(4, 80, 2, 128), (0, 2, 1, 3)).reshape(4, 2, 1, NLON)
    return grid, sums.reshape(ng * 4, width)


def solution(mesh):
    in_specs = (
        P("basin", None, "wave", None),
        P("wave", None, None),
        P("wave"),
        P("wave", None),
        P("wave", None, None),
        P("wave", None),
    )
    out_specs = (P("basin", None, "wave", None), P(None, ("wave", "basin")))
    return jax.shard_map(
        per_device, mesh=mesh, in_specs=in_specs, out_specs=out_specs, check_vma=False
    )
```

```python
import functools
import math

import jax
import jax.numpy as jnp
from jax import lax
from jax.experimental import pallas as pl
from jax.experimental.pallas import tpu as pltpu
from jax.sharding import PartitionSpec as P

NLON = 10240
LB = 128
BLOCK = 128
SLOTS = 16
BPW_BITS = 9
BPW = 1 << BPW_BITS
MESH = pl.DeviceIdType.MESH
F32 = jnp.float32
BF16 = jnp.bfloat16

COS_C = [(-1) ** n * math.pi ** (2 * n) / math.factorial(2 * n) for n in range(7)]
SIN_C = [(-1) ** n * math.pi ** (2 * n + 1) / math.factorial(2 * n + 1) for n in range(6)]


def cos_sin(r, turn):
    r = r - turn * jnp.floor(r * (1.0 / turn) + 0.5)
    y = r * (1.0 / turn)
    yy = y * y
    c = jnp.full_like(yy, COS_C[6])
    for k in range(5, -1, -1):
        c = c * yy + COS_C[k]
    s = jnp.full_like(yy, SIN_C[5])
    for k in range(4, -1, -1):
        s = s * yy + SIN_C[k]
    s = s * y
    return 1.0 - 2.0 * (s * s), 2.0 * (s * c)


def each_other(me, nw, act, between=lambda: None):
    if nw != 128:
        between()
        lax.fori_loop(1, nw, lambda k, carry: (act(lax.rem(me + k, nw)), carry)[1], 0)
        return
    x, z, c = me >> 5, (me >> 1) & 15, me & 1
    planes = [(((x + xd) & 3) << 5) | (c ^ cd) for xd in (2, 1, 3, 0) for cd in (1, 0)]

    def level(i, carry):
        there = ((z + 8 + ((i + 1) >> 1) * (2 * (i & 1) - 1)) & 15) << 1
        for plane in planes:
            act(plane | there)
        return carry

    lax.fori_loop(0, 5, level, 0)
    between()
    lax.fori_loop(5, 15, level, 0)
    for plane in planes[:-1]:
        act(plane | (z << 1))


def iota(shape, dim):
    return lax.broadcasted_iota(jnp.int32, shape, dim)


def kernel(nw, ng, spec_hbm, leg_hbm, wn_hbm, blk_hbm, wgt_hbm, bas_hbm,
           grid_hbm, sums_ref,
           spec_ref, wn_ref, blk_ref, wgt_ref, bas_ref, leg, sa, ra, sb, rb, sd, rd, tu, ba, ca, sn, ws, key, one, vs, gr, spread, sm,
           in_sem, leg_sem, grid_sem, sa_sem, ra_sem, sb_sem, rb_sem, sd_sem, rd_sem):
    me, y = lax.axis_index("wave"), lax.axis_index("basin")
    mloc = leg.shape[0]
    nb, eb = bas_ref.shape
    nq = SLOTS * nw

    barrier = pltpu.get_barrier_semaphore()

    def greet(to):
        pl.semaphore_signal(barrier, inc=1, device_id=(to, y), device_id_type=MESH)

    bring = [pltpu.make_async_copy(*pair, in_sem.at[i]) for i, pair in enumerate((
        (bas_hbm, bas_ref), (spec_hbm, spec_ref), (wn_hbm, wn_ref), (blk_hbm, blk_ref),
        (wgt_hbm, wgt_ref)))]

    def load():
        for copy in bring[:2]:
            copy.start()
        for m in range(mloc):
            pltpu.make_async_copy(leg_hbm.at[m], leg.at[m], leg_sem.at[m]).start()
        for copy in bring[2:]:
            copy.start()

    each_other(me, nw, greet, load)
    for k in range(1, ng):
        pl.semaphore_signal(barrier, inc=1, device_id=(me, lax.rem(y + k, ng)), device_id_type=MESH)

    bring[0].wait()
    bas = bas_ref[...]
    owner = bas >> BPW_BITS
    local = bas & (BPW - 1)
    upper = (iota((eb, eb), 0) < iota((eb, eb), 1)).astype(F32).astype(BF16)
    owned = [(owner[i:i + 1] == iota((nw, eb), 0)).astype(F32) for i in range(nb)]
    before = jnp.zeros((nw, 1), F32)
    ranks = []
    for i in range(nb):
        inside = jnp.dot(owned[i].astype(BF16), upper, preferred_element_type=F32)
        ranks.append(jnp.sum(owned[i] * (inside + before), axis=0, keepdims=True))
        before = before + jnp.sum(owned[i], axis=1, keepdims=True)
    lane = iota((128, eb), 0)
    where_to = jnp.zeros((nw, 128), F32)
    for i in range(nb):
        high = (local[i:i + 1] >> 7).astype(F32)
        low = (local[i:i + 1] & 127).astype(F32)
        rank = ranks[i].astype(jnp.int32)
        named = jnp.where(lane == rank + 96, high, 0.0) + jnp.where(lane == rank + 112, low, 0.0)
        where_to = where_to + lax.dot_general(
            owned[i].astype(BF16), named.astype(BF16), (((1,), (1,)), ((), ())),
            preferred_element_type=F32)
    rank_rows = jnp.concatenate(ranks, axis=0)
    place = rank_rows * float(nw) + owner.astype(F32)
    place_cols = jnp.transpose(place)

    ncoef = spec_ref.shape[3]
    odd = lax.rem(iota((8, ncoef), 1), 2) == 1
    bring[1].wait()

    def column(m, carry):
        rows = jnp.concatenate([spec_ref[f, m].astype(F32) for f in range(4)], axis=0)
        both = jnp.concatenate([rows, jnp.where(odd, -rows, rows)], axis=0).astype(BF16)
        pltpu.make_async_copy(leg_hbm.at[m], leg.at[m], leg_sem.at[m]).wait()
        sm[pl.ds(pl.multiple_of(m * 16, 16), 16)] = jnp.dot(
            both, leg[m], preferred_element_type=F32)
        return carry

    lax.fori_loop(0, mloc, column, 0)
    sums = sm[...]
    if mloc * 16 % 128:
        sums = jnp.concatenate([sums, jnp.zeros((256 - mloc * 16, nw), F32)], axis=0)
    by_lat = jnp.transpose(sums).astype(BF16)
    src = iota((256, 256), 0)
    dst = iota((256, 256), 1)
    r_of, lane_of = dst >> 7, dst & 127
    m_of, f_of, h_of = lane_of >> 3, (lane_of >> 1) & 3, lane_of & 1
    pick = (src == m_of * 16 + h_of * 8 + f_of * 2 + r_of) & (lane_of < mloc * 8)
    ordered = jnp.dot(by_lat, pick.astype(F32).astype(BF16), preferred_element_type=F32)
    lane = iota((1, 128), 1)
    numbers = jnp.zeros((1, 128), F32)
    bring[2].wait()
    for m in range(mloc):
        wn = wn_ref[m]
        chunk = (wn & 1) * 5 + (wn >> 8)
        numbers = numbers + jnp.where(lane == 80 + m, chunk.astype(F32), 0.0)
        numbers = numbers + jnp.where(lane == 96 + m, ((wn >> 1) & 127).astype(F32), 0.0)
    part_re = ordered[:, :128] + numbers
    part_im = ordered[:, 128:] + where_to
    sa[...] = jnp.concatenate([part_re[:, None, :], part_im[:, None, :]], axis=1).astype(BF16)

    pl.semaphore_wait(barrier, nw - 1 + ng - 1)

    def send_a(to):
        pltpu.make_async_remote_copy(
            src_ref=sa.at[pl.ds(to, 1)], dst_ref=ra.at[pl.ds(me, 1)], send_sem=sa_sem,
            recv_sem=ra_sem, device_id=(to, y), device_id_type=MESH).start()

    each_other(me, nw, send_a)
    ra[pl.ds(me, 1)] = sa[pl.ds(me, 1)]

    bring[3].wait()
    bring[4].wait()
    ext = jnp.concatenate(
        [jnp.concatenate([blk_ref[i:i + 1].astype(F32), jnp.zeros((15, eb), F32)], axis=0)
         for i in range(nb)], axis=1)
    turned_w = jnp.concatenate(
        [jnp.transpose(wgt_ref[i * eb:(i + 1) * eb].astype(F32)) for i in range(nb)], axis=1)
    left = jnp.concatenate([turned_w, ext], axis=0).astype(BF16)
    qc = min(256, nq)
    for i in range(nb):
        spread[i * eb:(i + 1) * eb] = jnp.broadcast_to(place_cols[:, i:i + 1], (eb, qc))
    spot = iota((1, qc), 1).astype(F32)

    def put(c, carry):
        cols = pl.ds(pl.multiple_of(c * qc, qc), qc)
        placed = jnp.where(spread[...] == spot + (c * qc).astype(F32), 1.0, 0.0).astype(BF16)
        slots = jnp.dot(left, placed, preferred_element_type=F32)
        block = slots[128:129]
        south = jnp.where(block >= 80.0, 1.0, 0.0)
        a = block - 80.0 * south
        side = jnp.where(a >= 40.0, 1.0, 0.0)
        ws[:128, cols] = jnp.where(side == 0.0, slots[:128], 0.0).astype(BF16)
        ws[128:, cols] = jnp.where(side == 1.0, slots[:128], 0.0).astype(BF16)
        key[:, cols] = jnp.broadcast_to((a - 40.0 * side) * 2.0 + south, (8, qc))
        return carry

    lax.fori_loop(0, nq // qc, put, 0)

    a_of = (iota((40, 128), 0) >> 1).astype(F32)
    lane_of = iota((1, 128), 1).astype(F32)
    m_of, b_of = iota((128, LB), 0).astype(F32), iota((128, LB), 1).astype(F32)
    flip = 1.0 - 2.0 * (iota((128, LB), 0) & 1).astype(F32)

    def table(k, carry):
        is_odd = k >= 5
        odd_one = is_odd.astype(jnp.int32)
        first = ((k - 5 * odd_one) * 256 + odd_one).astype(F32)
        number = 2.0 * lane_of + first
        weight = jnp.where(number == 0.0, 1.0, 2.0)
        cos_a, sin_a = cos_sin(number * a_of, 80.0)
        ca[k], sn[k] = cos_a * weight, sin_a * weight
        cos_b, sin_b = cos_sin((2.0 * m_of + first) * b_of, float(NLON))
        row = pl.multiple_of(k * 256, 256)
        ba[pl.ds(row, 128), :128] = cos_b.astype(BF16)
        ba[pl.ds(row + 128, 128), :128] = (-sin_b).astype(BF16)
        ba[pl.ds(row, 128), 128:] = (jnp.where(is_odd, -sin_b, cos_b) * flip).astype(BF16)
        ba[pl.ds(row + 128, 128), 128:] = (jnp.where(is_odd, -cos_b, -sin_b) * flip).astype(BF16)
        return carry

    lax.fori_loop(0, 10, table, 0)

    pltpu.make_async_copy(sa.at[pl.ds(0, nw - 1)], ra.at[pl.ds(0, nw - 1)], ra_sem).wait()

    got = ra[...].astype(F32)
    re, im = got[:, 0, :], got[:, 1, :]
    re_t, im_t = jnp.transpose(re), jnp.transpose(im)
    low_row = iota((128, nw), 0).astype(F32)
    lefts, rights = [], []
    for m in range(mloc):
        both = jnp.concatenate([re_t[m * 8:(m + 1) * 8], im_t[m * 8:(m + 1) * 8]], axis=0)
        high = re_t[80 + m:81 + m]
        lefts.append(jnp.concatenate(
            [jnp.where(high == float(hi), both, 0.0) for hi in range(10)], axis=0).astype(BF16))
        rights.append(jnp.where(re_t[96 + m:97 + m] == low_row, 1.0, 0.0).astype(BF16))
    columns = lax.dot_general(
        jnp.concatenate(lefts, axis=1), jnp.concatenate(rights, axis=1), (((1,), (1,)), ((), ())),
        preferred_element_type=F32)

    parity = (iota((8, 128), 0) & 1) == 0
    for k in range(10):
        cos_a, sin_a = ca[k].reshape(5, 8, 128), sn[k].reshape(5, 8, 128)
        g_re, g_im = columns[k * 16:k * 16 + 8], columns[k * 16 + 8:k * 16 + 16]
        for f in range(4):
            fr = jnp.where(parity, g_re[2 * f:2 * f + 1], g_re[2 * f + 1:2 * f + 2])[None]
            fi = jnp.where(parity, g_im[2 * f:2 * f + 1], g_im[2 * f + 1:2 * f + 2])[None]
            t_re = (fr * cos_a - fi * sin_a).reshape(40, 128)
            t_im = (fr * sin_a + fi * cos_a).reshape(40, 128)
            tu[k // 5, f * 40:(f + 1) * 40, k % 5 * 256:k % 5 * 256 + 128] = t_re.astype(BF16)
            tu[k // 5, f * 40:(f + 1) * 40, k % 5 * 256 + 128:k % 5 * 256 + 256] = t_im.astype(BF16)
    scale = 1.0 / math.sqrt(2.0 * mloc * nw)
    even = jnp.dot(tu[0], ba[:1280], preferred_element_type=F32)
    odd = jnp.dot(tu[1], ba[1280:], preferred_element_type=F32)
    plus, minus = (even + odd) * scale, (even - odd) * scale
    for f in range(4):
        rows = slice(f * 40, (f + 1) * 40)
        for side, lines in enumerate((plus, minus)):
            gr[f, side * 80:(side + 1) * 80] = jnp.concatenate(
                [lines[rows, :128], lines[rows, 128:]], axis=0).astype(BF16)

    row = iota((80, qc), 0).astype(F32)
    sides = jnp.concatenate(
        [jnp.concatenate([gr[f, :80], gr[f, 80:]], axis=1) for f in range(4)], axis=0)
    for c in range(nq // qc):
        cols = slice(c * qc, (c + 1) * qc)
        hit = row == key[0:1, cols]
        prod = jnp.dot(sides, ws[:, cols], preferred_element_type=F32)
        val = jnp.concatenate(
            [jnp.sum(jnp.where(hit, prod[f * 80:(f + 1) * 80], 0.0), axis=0, keepdims=True)
             for f in range(4)], axis=0)
        high = val.astype(BF16).astype(F32)
        val = jnp.concatenate([high, val - high], axis=0)
        for j in range(qc // nw):
            s = c * (qc // nw) + j
            vs[s * 8:(s + 1) * 8] = val[:, j * nw:(j + 1) * nw]
    sb[...] = jnp.transpose(vs[...])

    def send_b(to):
        pltpu.make_async_remote_copy(
            src_ref=sb.at[pl.ds(to, 1)], dst_ref=rb.at[pl.ds(me, 1)], send_sem=sb_sem,
            recv_sem=rb_sem, device_id=(to, y), device_id_type=MESH).start()

    each_other(me, nw, send_b)
    rb[pl.ds(me, 1)] = sb[pl.ds(me, 1)]
    out = pltpu.make_async_copy(gr, grid_hbm, grid_sem)
    out.start()

    for s in range(SLOTS):
        one[:, s * nw:(s + 1) * nw] = jnp.where(
            im_t[112 + s:113 + s] == low_row, 1.0, 0.0).astype(BF16)

    pltpu.make_async_copy(sb.at[pl.ds(0, nw - 1)], rb.at[pl.ds(0, nw - 1)], rb_sem).wait()
    val = jnp.transpose(rb[...])
    named = []
    for s in range(SLOTS):
        high = im_t[96 + s:97 + s]
        named.append(jnp.concatenate(
            [jnp.where(high == float(hi), val[s * 8:(s + 1) * 8], 0.0) for hi in range(BPW // 128)],
            axis=0).astype(BF16))
    dense = lax.dot_general(jnp.concatenate(named, axis=1), one[...], (((1,), (1,)), ((), ())),
                            preferred_element_type=F32)
    dense = [dense[hi * 8:hi * 8 + 4] + dense[hi * 8 + 4:hi * 8 + 8] for hi in range(BPW // 128)]
    each = BPW // 128 // ng
    for g in range(ng):
        for k in range(each):
            sd[g, :, k * 128:(k + 1) * 128] = dense[g * each + k]
    moves = []
    for k in sorted(range(1, ng), key=lambda k: abs(2 * k - ng)):
        to = lax.rem(y + k, ng)
        moves.append(pltpu.make_async_remote_copy(
            src_ref=sd.at[to], dst_ref=rd.at[y], send_sem=sd_sem, recv_sem=rd_sem,
            device_id=(me, to), device_id_type=MESH))
        moves[-1].start()
    rd[y] = sd[y]
    pltpu.make_async_copy(sd.at[pl.ds(0, ng - 1)], rd.at[pl.ds(0, ng - 1)], rd_sem).wait()
    sums_ref[...] = rd[...]

    out.wait()
    pltpu.make_async_copy(sa.at[pl.ds(0, nw - 1)], ra.at[pl.ds(0, nw - 1)], sa_sem).wait()
    pltpu.make_async_copy(sb.at[pl.ds(0, nw - 1)], rb.at[pl.ds(0, nw - 1)], sb_sem).wait()
    pltpu.make_async_copy(sd.at[pl.ds(0, ng - 1)], rd.at[pl.ds(0, ng - 1)], sd_sem).wait()


def per_device(spectra, legendre, wave_numbers, block_index, block_weights, basin_index):
    nw, ng = lax.axis_size("wave"), lax.axis_size("basin")
    mloc, ncoef, lats = legendre.shape
    nnz = block_index.shape[1]
    eb = min(128, nnz)
    nq = SLOTS * nw
    width = BPW // ng
    vmem = pl.BlockSpec(memory_space=pltpu.VMEM)
    grid, sums = pl.pallas_call(
        functools.partial(kernel, nw, ng),
        out_shape=(jax.ShapeDtypeStruct((4, 160, 128), BF16),
                   jax.ShapeDtypeStruct((ng, 4, width), F32)),
        in_specs=[pl.BlockSpec(memory_space=pltpu.HBM)] * 6,
        out_specs=(pl.BlockSpec(memory_space=pl.ANY), vmem),
        scratch_shapes=[
            pltpu.VMEM((4, mloc, 2, ncoef), BF16),
            pltpu.SMEM((mloc,), jnp.int32),
            pltpu.VMEM((nnz // eb, eb), jnp.int32),
            pltpu.VMEM((nnz, BLOCK), BF16),
            pltpu.VMEM((nnz // eb, eb), jnp.int32),
            pltpu.VMEM((mloc, ncoef, lats), BF16),
            pltpu.VMEM((nw, 2, 128), BF16),
            pltpu.VMEM((nw, 2, 128), BF16),
            pltpu.VMEM((nw, 128), F32),
            pltpu.VMEM((nw, 128), F32),
            pltpu.VMEM((ng, 4, width), F32),
            pltpu.VMEM((ng, 4, width), F32),
            pltpu.VMEM((2, 160, 1280), BF16),
            pltpu.VMEM((2560, 256), BF16),
            pltpu.VMEM((10, 40, 128), F32),
            pltpu.VMEM((10, 40, 128), F32),
            pltpu.VMEM((256, nq), BF16),
            pltpu.VMEM((8, nq), F32),
            pltpu.VMEM((128, nq), BF16),
            pltpu.VMEM((128, nw), F32),
            pltpu.VMEM((4, 160, 128), BF16),
            pltpu.VMEM((nnz, min(256, nq)), F32),
            pltpu.VMEM((16 * mloc, nw), F32),
            pltpu.SemaphoreType.DMA((5,)),
            pltpu.SemaphoreType.DMA((mloc,)),
            pltpu.SemaphoreType.DMA,
            pltpu.SemaphoreType.DMA,
            pltpu.SemaphoreType.DMA,
            pltpu.SemaphoreType.DMA,
            pltpu.SemaphoreType.DMA,
            pltpu.SemaphoreType.DMA,
            pltpu.SemaphoreType.DMA,
        ],
        compiler_params=pltpu.CompilerParams(
            collective_id=0, has_side_effects=True, vmem_limit_bytes=40 * 1024 * 1024),
    )(*[pltpu.with_memory_space_constraint(x, pltpu.HBM) for x in (
        jnp.transpose(spectra, (0, 2, 1, 3)), legendre, wave_numbers,
        block_index.reshape(nnz // eb, eb), block_weights.reshape(nnz, BLOCK),
        basin_index.reshape(nnz // eb, eb))])
    grid = jnp.transpose(grid.reshape(4, 80, 2, 128), (0, 2, 1, 3)).reshape(4, 2, 1, NLON)
    return grid, sums.reshape(ng * 4, width)


def solution(mesh):
    in_specs = (
        P("basin", None, "wave", None),
        P("wave", None, None),
        P("wave"),
        P("wave", None),
        P("wave", None, None),
        P("wave", None),
    )
    out_specs = (P("basin", None, "wave", None), P(None, ("wave", "basin")))
    return jax.shard_map(
        per_device, mesh=mesh, in_specs=in_specs, out_specs=out_specs, check_vma=False
    )
```
